256 devices in a mesh: ctx: 64 (over x, z, core), head: 4 (over y).
Axes of the slice: x: 4, y: 4, z: 8, core: 2. Of those that a mesh axis runs over, the one named last changes fastest.
Arguments:
- queries: bfloat16 [8192, 1536], P('ctx', 'head'), may hold values from -16 to 16
- key_rows: bfloat16 [8192, 1536], P('ctx', 'head'), may hold values from -6 to 6
- value_rows: bfloat16 [8192, 1536], P('ctx', 'head'), may hold values from -6 to 6
- out_weight: bfloat16 [3072, 1536], P(None, 'head'), may hold values from -0.15625 to 0.15625
- grad_projected: bfloat16 [8192, 3072], P('ctx', 'head'), may hold values from -16 to 16
- segment_len: int32 [8], replicated, may hold values from 1 to 2048, 8192 in all
- block_order: int32 [128], replicated, may hold values from 0 to 127, each once
Outputs:
- projected: bfloat16 [8192, 3072], P('ctx', 'head')
- grad_queries: bfloat16 [8192, 1536], P('ctx', 'head')
- grad_keys: bfloat16 [8192, 1536], P('ctx', 'head')
- grad_values: bfloat16 [8192, 1536], P('ctx', 'head')
- grad_out_weight: float32 [3072, 1536], P('ctx', 'head')
The draws below stay inside these ranges and needn't reach their ends.
Inputs may be any that keep to these rules, and one draw needn't show every extreme that they name: `segment_len`: the lengths sum to 8192; the longest is exactly 2048. `block_order`: each block index appears once.
All inputs are finite; a program needn't handle non-finite values.
Results may differ from the reference program's by a relative error of at most 0.04.
Values may be sent and summed in bfloat16 or wider, within the bound.
A program may use at most 128 MiB of HBM per device.

```python
import math
import jax
import jax.numpy as jnp
import numpy as np
from jax import lax

D = 3072
HEADS = 12
HD = 128
SEGMENTS = 8
TOK_DEV = 128
TOKENS = 8192
BLK = 64
NBLK = 128
N_HEAD = 4


def draw_queries(key, part):
    key = jax.random.fold_in(key, 1)
    drawn = jnp.clip(jax.random.normal(key, (TOKENS, HEADS * HD), jnp.float32), -6.0, 6.0)
    return drawn.astype(jnp.bfloat16)


def draw_key_rows(key, part):
    key = jax.random.fold_in(key, 2)
    drawn = jnp.clip(jax.random.normal(key, (TOKENS, HEADS * HD), jnp.float32), -6.0, 6.0)
    return drawn.astype(jnp.bfloat16)


def with_spikes(result, key, source, target, parts, factor):
    owner, partner = [(jnp.arange(result.shape[axis_at]) // (result.shape[axis_at] // parts)).reshape([-1 if axis == axis_at else 1 for axis in range(result.ndim)]) for axis_at in (source, target)]
    chosen = jax.random.permutation(key, parts)[partner]
    strong = (owner == chosen) | (owner == (partner + parts // 2) % parts)
    return jnp.where(strong, factor * result, result)


def block_levels(own_key, extent, shards, smallest, largest):
    factor_of = 1.0
    for dim, parts in shards:
        draws = jax.random.uniform(jax.random.fold_in(jax.random.fold_in(own_key, 6), dim), (parts,), jnp.float32, smallest / len(shards), largest / len(shards))
        factor_of = factor_of * jnp.repeat(jnp.exp(draws), extent[dim] // parts).reshape((-1,) + (1,) * (len(extent) - 1 - dim))
    return factor_of


def profile(amount, total, bound, lean):
    weights = [(1 << 20) // math.isqrt(standing ** lean) + 1 for standing in range(2, amount + 1)]
    rest, given = total - bound - (amount - 1), [1] * (amount - 1)
    while rest > 0:
        free = [i for i in range(amount - 1) if given[i] < bound]
        mass, budget = sum([weights[i] for i in free]), rest
        for i in free:
            extra = min(bound - given[i], max(1, budget * weights[i] // mass), rest)
            given[i] = given[i] + extra
            rest = rest - extra
    return np.array([bound] + given)


def ragged_sizes(stream_key, count, total, bound, lean):
    if count == 2:
        one = jax.random.randint(stream_key, (), max(1, total - bound), min(bound, total - 1) + 1)
        return jnp.stack([one, total - one])
    tallies = jnp.asarray(profile(count, total, bound, lean), jnp.int32)
    pairs = (count - 1) // 2
    source_of, sink = tallies[1:1 + 2 * pairs:2], tallies[2:2 + 2 * pairs:2]
    margin = jnp.minimum(source_of - 1, bound - sink)
    shifted = jax.random.randint(jax.random.fold_in(stream_key, 1), (pairs,), 0, 1 << 20) % (margin + 1)
    tallies = tallies.at[1:1 + 2 * pairs:2].set(source_of - shifted).at[2:2 + 2 * pairs:2].set(sink + shifted)
    return tallies[jax.random.permutation(jax.random.fold_in(stream_key, 2), count)]


def gaussian(own_key, dims, deviation, limit, shards=(), kind=jnp.bfloat16):
    values = deviation * jax.random.normal(own_key, dims, jnp.float32)
    if shards:
        values = values * block_levels(own_key, dims, shards, -0.22, 0.18)
    return jnp.clip(values, -limit, limit).astype(kind)


def heavy_noise(rng, shape, spread, limit, split, heavy, kind=jnp.bfloat16):
    result = spread * jax.random.normal(rng, shape, jnp.float32)
    if split:
        result = result * block_levels(rng, shape, split, -0.22, 0.18)
    return jnp.clip(with_spikes(result, jax.random.fold_in(rng, 3), *heavy), -limit, limit).astype(kind)


def setup_inputs(seed: int = 0) -> dict:
    arg_keys = jax.random.split(jax.random.key(seed), 8)
    queries = draw_queries(jax.random.fold_in(arg_keys[7], 71), 0)
    key_rows = draw_key_rows(jax.random.fold_in(arg_keys[7], 71), 0)
    value_rows = gaussian(arg_keys[2], (TOKENS, HEADS * HD), 1.0, 6.0, ((0, 64), (1, 4)))
    out_weight = gaussian(arg_keys[3], (D, HEADS * HD), (HEADS * HD) ** -0.5, 0.15625, ((1, 4),))
    grad_projected = heavy_noise(arg_keys[4], (TOKENS, D), 1.0, 16.0, ((0, 64), (1, 4)), (0, 1, 64, 4.0))
    segment_len = ragged_sizes(arg_keys[5], SEGMENTS, TOKENS, TOKENS // 4, 1).astype(jnp.int32)
    block_order = jax.random.permutation(arg_keys[6], NBLK).astype(jnp.int32)
    return dict(queries=queries, key_rows=key_rows, value_rows=value_rows, out_weight=out_weight, grad_projected=grad_projected, segment_len=segment_len, block_order=block_order)


NEG_FILL = -1e+30

def segment_ids(segment_len, block_order):
    row_ids = jnp.arange(TOKENS, dtype=jnp.int32)
    position = block_order[row_ids // BLK].astype(jnp.int32) * BLK + row_ids % BLK
    seg_ends = jnp.cumsum(segment_len).astype(jnp.int32)
    return lax.optimization_barrier(jnp.sum((position[:, None] >= seg_ends[None, :]).astype(jnp.int32), axis=1))

def reference(queries, key_rows, value_rows, out_weight, grad_projected, segment_len, block_order):
    scaling = 1.0 / math.sqrt(HD)
    segment = segment_ids(segment_len, block_order)
    dout = jnp.dot(grad_projected, out_weight, preferred_element_type=jnp.float32).astype(jnp.bfloat16)

    def by_head(array_in):
        return array_in.reshape(TOKENS, HEADS, HD).transpose(1, 0, 2)
    blocks = TOKENS // TOK_DEV

    def per_head(arrays):
        query_head, key_head, value_head, dout_head = arrays

        def query_block(block_idx):
            first_row = block_idx * TOK_DEV
            query_blk = lax.dynamic_slice_in_dim(query_head, first_row, TOK_DEV, 0)
            dout_blk = lax.dynamic_slice_in_dim(dout_head, first_row, TOK_DEV, 0)
            seg_blk = lax.dynamic_slice_in_dim(segment, first_row, TOK_DEV, 0)
            scores = jnp.dot(query_blk, key_head.T, preferred_element_type=jnp.float32) * scaling
            visible = segment[None, :] <= seg_blk[:, None]
            scores = jnp.where(visible, scores, NEG_FILL)
            maxima = lax.optimization_barrier(jnp.max(scores, axis=1))
            weights = jnp.where(visible, jnp.exp(scores - maxima[:, None]), 0.0)
            totals = lax.optimization_barrier(jnp.sum(weights, axis=1))
            probs = weights / totals[:, None]
            output = jnp.dot(probs.astype(jnp.bfloat16), value_head, preferred_element_type=jnp.float32)
            delta = lax.optimization_barrier(jnp.sum(dout_blk.astype(jnp.float32) * output, axis=1))
            grad_prob = jnp.dot(dout_blk, value_head.T, preferred_element_type=jnp.float32)
            grad_score = (probs * (grad_prob - delta[:, None])).astype(jnp.bfloat16)
            grad_query = scaling * jnp.dot(grad_score, key_head, preferred_element_type=jnp.float32)
            return (output, maxima + jnp.log(totals), delta, grad_query)
        output, row_lse, delta, grad_query = lax.map(query_block, jnp.arange(blocks, dtype=jnp.int32))
        output = output.reshape(TOKENS, HD)
        row_lse = row_lse.reshape(TOKENS)
        delta = delta.reshape(TOKENS)
        grad_query = grad_query.reshape(TOKENS, HD)

        def key_block(block_idx):
            first_row = block_idx * TOK_DEV
            key_blk = lax.dynamic_slice_in_dim(key_head, first_row, TOK_DEV, 0)
            value_blk = lax.dynamic_slice_in_dim(value_head, first_row, TOK_DEV, 0)
            seg_blk = lax.dynamic_slice_in_dim(segment, first_row, TOK_DEV, 0)
            scores = jnp.dot(key_blk, query_head.T, preferred_element_type=jnp.float32) * scaling
            visible = seg_blk[:, None] <= segment[None, :]
            probs = jnp.exp(jnp.where(visible, scores - row_lse[None, :], NEG_FILL))
            grad_value = jnp.dot(probs.astype(jnp.bfloat16), dout_head, preferred_element_type=jnp.float32)
            grad_prob = jnp.dot(value_blk, dout_head.T, preferred_element_type=jnp.float32)
            grad_score = (probs * (grad_prob - delta[None, :])).astype(jnp.bfloat16)
            grad_key = scaling * jnp.dot(grad_score, query_head, preferred_element_type=jnp.float32)
            return (grad_key, grad_value)
        grad_key, grad_value = lax.map(key_block, jnp.arange(blocks, dtype=jnp.int32))
        return (output, grad_query, grad_key.reshape(TOKENS, HD), grad_value.reshape(TOKENS, HD))
    outputs = lax.map(per_head, (by_head(queries), by_head(key_rows), by_head(value_rows), by_head(dout)))

    def to_rows(array_in):
        return array_in.transpose(1, 0, 2).reshape(TOKENS, HEADS * HD)
    attended = to_rows(outputs[0]).astype(jnp.bfloat16)
    group_span = HEADS // N_HEAD * HD
    summed = jnp.zeros((TOKENS, D), jnp.float32)
    for group in range(N_HEAD):
        partial_proj = jnp.dot(attended[:, group * group_span:(group + 1) * group_span], out_weight[:, group * group_span:(group + 1) * group_span].T, preferred_element_type=jnp.float32).astype(jnp.bfloat16)
        partial_proj = lax.optimization_barrier(partial_proj)
        summed = summed + partial_proj.astype(jnp.float32)
    projected = summed.astype(jnp.bfloat16)
    grad_out_weight = jnp.dot(grad_projected.T, attended, preferred_element_type=jnp.float32)
    return (projected, to_rows(outputs[1]).astype(jnp.bfloat16), to_rows(outputs[2]).astype(jnp.bfloat16), to_rows(outputs[3]).astype(jnp.bfloat16), grad_out_weight)
```

```python
import functools
import math

import jax
import jax.numpy as jnp
from jax import lax
from jax.experimental import pallas as pl
from jax.experimental.pallas import tpu as pltpu
from jax.sharding import PartitionSpec as P

HD = 128
HEADS = 3
TOK = 128
WID = HEADS * HD
BLK = 64
SEGS = 8
SCALE = 1.0 / math.sqrt(HD)
EXP2_SCALE = SCALE * math.log2(math.e)
NEG_FILL = -1e30
MAX_FLOOR = -1e20
F32 = jnp.float32
BF16 = jnp.bfloat16
MESH = pl.DeviceIdType.MESH


def dot_nn(a, b):
    return jnp.dot(a, b, preferred_element_type=F32)


def dot_nt(a, b):
    return lax.dot_general(a, b, (((1,), (1,)), ((), ())), preferred_element_type=F32)


def dot_tn(a, b):
    return lax.dot_general(a, b, (((0,), (0,)), ((), ())), preferred_element_type=F32)


def head_lanes(h):
    return pl.ds(pl.multiple_of(h * HD, HD), HD)


def kernel(
    X, Z, Y,
    seg_len, order, q_in, k_in, v_in, w_in, gp_in,
    proj_out, dq_out, dk_out, dv_out, gw_out,
    qb, db, kvb, gpf, gpx, segk, segq, pbuf, dpbuf, mst, lst, dst,
    oacc, mrun, st_send, st_recv, o_send, o_recv, attb, dqacc, dq_send, dq_recv,
    pj_send, pj_recv, fac, delta, part, sib_recv, rs_send, rs_recv,
    gwf, gwp, g_sib, g_send, g_recv,
    x_ss, x_rs, y_ss, y_rs, ring_ss, ring_rs, ksib_ss, ksib_rs,
    sib_ss, sib_rs, rs_ss, rs_rs, gsib_ss, gsib_rs, g_ss, g_rs,
):
    nplus, nminus = Z // 2, Z - 1 - Z // 2
    QN = X * TOK
    gcols = gp_in.shape[1]
    me = lax.axis_index("ctx")
    y = lax.axis_index("head")
    core = lax.rem(me, 2)
    z = lax.rem(me // 2, Z)
    x = me // (2 * Z)

    def ctx_of(xx, zz, cc):
        return (xx * Z + zz) * 2 + cc

    def zmod(off):
        return lax.rem(z + off + 2 * Z, Z)

    other = 1 - core
    sib = (ctx_of(x, z, other), y)
    up = (ctx_of(x, zmod(1), core), y)
    down = (ctx_of(x, zmod(-1), core), y)

    def x_dev(i):
        return (ctx_of(lax.rem(x + i, X), z, core), y)

    def y_dev(i):
        return (me, lax.rem(y + i, Y))

    def rcopy(src, dst_ref, ss, rs, dev):
        return pltpu.make_async_remote_copy(
            src_ref=src, dst_ref=dst_ref, send_sem=ss, recv_sem=rs,
            device_id=dev, device_id_type=MESH,
        )

    barrier = pltpu.get_barrier_semaphore()
    partners = [up, down, sib]
    partners += [x_dev(i) for i in range(1, X)] + [y_dev(i) for i in range(1, Y)]
    for dev in partners:
        pl.semaphore_signal(barrier, inc=1, device_id=dev, device_id_type=MESH)
    pl.semaphore_wait(barrier, len(partners))

    sends = []

    def go(copy):
        copy.start()
        sends.append(copy)

    def x_recv(kind, i, buf):
        slot = buf.at[lax.rem(x + X - i, X)]
        rcopy(slot, slot, x_ss.at[kind, i], x_rs.at[kind, i], x_dev(i)).wait_recv()

    def x_send(kind, i, src, buf):
        go(rcopy(src, buf.at[x], x_ss.at[kind, i], x_rs.at[kind, i], x_dev(i)))

    def y_recv(kind, i, buf):
        slot = buf.at[lax.rem(y + Y - i, Y)]
        rcopy(slot, slot, y_ss.at[kind, i], y_rs.at[kind, i], y_dev(i)).wait_recv()

    def y_send(kind, i, src, buf):
        go(rcopy(src, buf.at[y], y_ss.at[kind, i], y_rs.at[kind, i], y_dev(i)))

    def kv_slot(off, cc, a):
        return kvb.at[zmod(off), cc, a]

    def ring_send(direction, step, a, src):
        off = 1 - step if direction == 0 else step - 1
        go(rcopy(
            src, kv_slot(off, core, a),
            ring_ss.at[direction, step - 1, a], ring_rs.at[direction, step - 1, a],
            up if direction == 0 else down,
        ))

    def ring_wait(direction, step, a):
        off = -step if direction == 0 else step
        slot = kv_slot(off, core, a)
        rcopy(
            slot, slot, ring_ss.at[direction, step - 1, a],
            ring_rs.at[direction, step - 1, a], up,
        ).wait_recv()

    def sib_index(off):
        return nplus + off if off > 0 else -off

    def ksib_send(off, a, src):
        j = sib_index(off)
        go(rcopy(src, kv_slot(off, core, a), ksib_ss.at[j, a], ksib_rs.at[j, a], sib))

    def ksib_wait(off, a):
        j = sib_index(off)
        slot = kv_slot(off, other, a)
        rcopy(slot, slot, ksib_ss.at[j, a], ksib_rs.at[j, a], sib).wait_recv()

    for i in range(1, Y):
        y_send(0, i, gp_in, gpf)
    for a, src in ((0, k_in), (1, v_in)):
        ring_send(0, 1, a, src)
        if nminus >= 1:
            ring_send(1, 1, a, src)
        ksib_send(0, a, src)
    for i in range(1, X):
        x_send(0, i, q_in, qb)
    qb[x] = q_in[...]
    kvb[z, core, 0] = k_in[...]
    kvb[z, core, 1] = v_in[...]

    ends = []
    total = seg_len[0]
    for i in range(SEGS - 1):
        ends.append(total)
        total = total + seg_len[i + 1]

    def segments(row_in_block, ctx_id):
        first = order[2 * ctx_id] * BLK
        second = order[2 * ctx_id + 1] * BLK - BLK
        pos = row_in_block + jnp.where(row_in_block < BLK, first, second)
        seg = jnp.zeros_like(pos)
        for end in ends:
            seg = seg + jnp.where(pos >= end, 1, 0)
        return seg

    lanes = lax.broadcasted_iota(jnp.int32, (1, TOK), 1)
    for xx in range(X):
        segq[:, xx * TOK:(xx + 1) * TOK] = segments(lanes, ctx_of(xx, z, core))
    rows = lax.broadcasted_iota(jnp.int32, (TOK, 128), 0)

    def seg_body(zz, carry):
        for cc in range(2):
            segk[zz, cc * TOK:(cc + 1) * TOK, :] = segments(rows, ctx_of(x, zz, cc))
        return carry

    lax.fori_loop(0, Z, seg_body, 0)
    for h in range(HEADS):
        mrun[h] = jnp.full((1, QN), MAX_FLOOR, F32)
        oacc[h] = jnp.zeros((HD, QN), F32)
        dqacc[h] = jnp.zeros((HD, QN), F32)

    def keys(zi, a, h):
        return kvb[zi, :, a, :, head_lanes(h)].reshape(2 * TOK, HD)

    def gathered(buf, h):
        return buf[:, :, head_lanes(h)].reshape(QN, HD)

    def fwd(zi):
        def body(h, carry):
            s = dot_nt(keys(zi, 0, h), gathered(qb, h))
            sk = jnp.concatenate([segk[zi]] * X, axis=1)
            s = jnp.where(sk <= segq[...], s, NEG_FILL)
            m = jnp.maximum(jnp.max(s, axis=0, keepdims=True), MAX_FLOOR)
            p = jnp.exp2((s - m) * EXP2_SCALE)
            pbuf[h, zi] = p
            mst[h, zi] = m
            lst[h, zi] = jnp.sum(p, axis=0, keepdims=True)
            pv = dot_tn(keys(zi, 1, h), p.astype(BF16))
            m_old = mrun[h]
            m_new = jnp.maximum(m_old, m)
            mrun[h] = m_new
            oacc[h] = (
                oacc[h] * jnp.exp2((m_old - m_new) * EXP2_SCALE)
                + pv * jnp.exp2((m - m_new) * EXP2_SCALE)
            )
            return carry

        lax.fori_loop(0, HEADS, body, 0)

    def dprob(zi):
        def body(h, carry):
            dp = dot_nt(keys(zi, 1, h), gathered(db, h))
            dpbuf[h, zi] = dp
            dst[h, zi] = jnp.sum(dp * pbuf[h, zi], axis=0, keepdims=True)
            return carry

        lax.fori_loop(0, HEADS, body, 0)

    def ring_step(step):
        for a in range(2):
            ring_wait(0, step, a)
            if step < nplus:
                ring_send(0, step + 1, a, kv_slot(-step, core, a))
            ksib_send(-step, a, kv_slot(-step, core, a))
            if step <= nminus:
                ring_wait(1, step, a)
                if step < nminus:
                    ring_send(1, step + 1, a, kv_slot(step, core, a))
                ksib_send(step, a, kv_slot(step, core, a))

    def step_offsets(step):
        return [0] if step == 0 else ([-step, step] if step <= nminus else [-step])

    def sib_ready(step):
        for off in step_offsets(step):
            for a in range(2):
                ksib_wait(off, a)

    def over(step, fn):
        offs = step_offsets(step)
        if len(offs) == 1:
            fn(zmod(offs[0]))
        else:
            def body(i, carry):
                fn(zmod(step * (2 * i - 1)))
                return carry

            lax.fori_loop(0, 2, body, 0)

    acc = None
    for i in range(Y):
        if i:
            y_recv(0, i, gpf)
        src_y = lax.rem(y + Y - i, Y)
        if i == 0:
            gpf[src_y] = gp_in[...]
        w_rows = w_in[pl.ds(pl.multiple_of(src_y * gcols, gcols), gcols), :]
        term = dot_nn(gpf[src_y], w_rows)
        acc = term if acc is None else acc + term
        if i == 0:
            ring_step(1)
    db[x] = acc.astype(BF16)
    for i in range(1, X):
        x_send(1, i, db.at[x], db)
    for i in range(1, X):
        x_send(2, i, gpf.at[lax.rem(x + i, X)], gpx)
    gpx[x] = gpf[x]

    for i in range(1, X):
        x_recv(0, i, qb)
    sib_ready(0)
    over(0, fwd)
    done = [0]
    have_dout = False
    for step in range(1, nplus + 1):
        sib_ready(step)
        if step < nplus:
            ring_step(step + 1)
        over(step, fwd)
        done.append(step)
        if step >= 2 and not have_dout:
            have_dout = True
            for i in range(1, X):
                x_recv(1, i, db)
            for prev in done:
                over(prev, dprob)
        elif have_dout:
            over(step, dprob)

    for h in range(HEADS):
        m_all, l_all, d_all = mst[h], lst[h], dst[h]
        m_top = mrun[h]
        w = jnp.exp2((m_all - m_top[None]) * EXP2_SCALE)
        l_sum = jnp.maximum(jnp.sum(l_all * w, axis=0), 1e-30)
        inv = 1.0 / l_sum
        st_send[h:h + 1, :] = m_top * EXP2_SCALE + jnp.log2(l_sum)
        st_send[HEADS + h:HEADS + h + 1, :] = jnp.sum(d_all * w, axis=0) * inv
        o_h = (oacc[h] * inv).astype(BF16)
        for xx in range(X):
            o_send[xx, h * HD:(h + 1) * HD, :] = o_h[:, xx * TOK:(xx + 1) * TOK]
    st_send[2 * HEADS:8, :] = jnp.zeros((8 - 2 * HEADS, QN), F32)
    for i in range(1, X):
        x_send(3, i, st_send, st_recv)
    for i in range(1, X):
        x_send(4, i, o_send.at[lax.rem(x + i, X)], o_recv)
    st_recv[x] = st_send[...]
    o_recv[x] = o_send[x]
    for i in range(1, X):
        x_recv(3, i, st_recv)
    lse_all = st_recv[:, 0:HEADS, :]
    top = jnp.max(lse_all, axis=0)
    lse = top + jnp.log2(jnp.sum(jnp.exp2(lse_all - top[None]), axis=0))
    weight = jnp.exp2(lse_all - lse[None])
    delta_all = jnp.sum(weight * st_recv[:, HEADS:2 * HEADS, :], axis=0)
    for h in range(HEADS):
        delta[h] = delta_all[h:h + 1]
        fac[h] = jnp.exp2(mst[h] * EXP2_SCALE - lse[h:h + 1][None])
    own_stats = st_recv[:, 0:HEADS, pl.ds(pl.multiple_of(x * TOK, TOK), TOK)]
    own_top = jnp.max(own_stats, axis=0)
    own_w = jnp.exp2(own_stats - own_top[None])
    own_w = own_w / jnp.sum(own_w, axis=0)[None]

    def dest_off(o):
        half = o // 2
        return jnp.where(lax.rem(o, 2) == 0, nplus - half, half - nminus)

    def bwd(o):
        zi = zmod(dest_off(o))

        def body(h, carry):
            lanes_h = head_lanes(h)
            p = pbuf[h, zi] * fac[h, zi]
            ds = (p * (dpbuf[h, zi] - delta[h])).astype(BF16)
            dv = dot_nn(p.astype(BF16), gathered(db, h)).astype(BF16)
            dk = (dot_nn(ds, gathered(qb, h)) * SCALE).astype(BF16)
            for cc in range(2):
                part[o, cc, 0, :, lanes_h] = dk[cc * TOK:(cc + 1) * TOK]
                part[o, cc, 1, :, lanes_h] = dv[cc * TOK:(cc + 1) * TOK]
            dqacc[h] = dqacc[h] + dot_tn(keys(zi, 0, h), ds)
            return carry

        lax.fori_loop(0, HEADS, body, 0)

    def sib_copy(o):
        return rcopy(part.at[o, other], sib_recv.at[o], sib_ss.at[o], sib_rs.at[o], sib)

    def ring_dev(o):
        zz = jnp.where(lax.rem(o, 2) == 0, zmod(1), zmod(-1))
        return (ctx_of(x, zz, core), y)

    def rs_copy(o):
        return rcopy(rs_send.at[o], rs_recv.at[o + 2], rs_ss.at[o], rs_rs.at[o + 2], ring_dev(o))

    def rs_wait(o):
        slot = rs_recv.at[o]
        rcopy(slot, slot, rs_ss.at[0], rs_rs.at[o], up).wait_recv()

    def finalize(o):
        sib_copy(o).wait_recv()
        for a in range(2):
            rs_send[o, a] = (
                part[o, core, a].astype(F32) + sib_recv[o, a].astype(F32)
            ).astype(BF16)

        @pl.when(o >= 2)
        def _():
            rs_wait(o)
            for a in range(2):
                rs_send[o, a] = (
                    part[o, core, a].astype(F32)
                    + sib_recv[o, a].astype(F32)
                    + rs_recv[o, a].astype(F32)
                ).astype(BF16)

        rs_copy(o).start()

    def bwd_range(first, last):
        def body(o, carry):
            bwd(o)
            sib_copy(o).start()
            finalize(o - 1)
            return carry

        lax.fori_loop(first, last, body, 0)

    cut_a, cut_b = max(1, Z // 4), max(2, Z // 2 + 1)
    bwd(0)
    sib_copy(0).start()
    bwd_range(1, cut_a)

    for i in range(1, X):
        x_recv(4, i, o_recv)
    for h in range(HEADS):
        o_t = jnp.zeros((HD, TOK), F32)
        for xx in range(X):
            o_t = o_t + o_recv[xx, h * HD:(h + 1) * HD, :].astype(F32) * own_w[xx, h:h + 1]
        attb[x, :, h * HD:(h + 1) * HD] = o_t.T.astype(BF16)
    for i in range(1, X):
        x_send(5, i, attb.at[x], attb)
    att = attb[x]
    for i in range(1, Y):
        dst_y = lax.rem(y + i, Y)
        w_rows = w_in[pl.ds(pl.multiple_of(dst_y * gcols, gcols), gcols), :]
        pj_send[dst_y] = dot_nt(att, w_rows).astype(BF16)
        y_send(1, i, pj_send.at[dst_y], pj_recv)
    w_rows = w_in[pl.ds(pl.multiple_of(y * gcols, gcols), gcols), :]
    pj_recv[y] = dot_nt(att, w_rows).astype(BF16)

    bwd_range(cut_a, cut_b)

    for i in range(1, X):
        x_recv(2, i, gpx)
    for i in range(1, X):
        x_recv(5, i, attb)
    att_all = attb[...].reshape(QN, WID)

    def gw_body(j, carry):
        lanes_j = pl.ds(pl.multiple_of(j * 128, 128), 128)
        left = gpx[:, :, lanes_j].reshape(QN, 128)
        gwf[pl.ds(pl.multiple_of(j * 128, 128), 128), :] = dot_tn(left, att_all)
        return carry

    lax.fori_loop(0, gcols // 128, gw_body, 0)
    grow = gw_out.shape[0]
    for zz in range(Z):
        for cc in range(2):
            first = (zz * 2 + cc) * grow
            gwp[cc, zz] = gwf[first:first + grow, :].astype(BF16)
    gsib = rcopy(gwp.at[other], g_sib, gsib_ss, gsib_rs, sib)
    go(gsib)

    bwd_range(cut_b, Z)

    for h in range(HEADS):
        dq_h = (dqacc[h] * SCALE).astype(BF16)
        for xx in range(X):
            dq_send[xx, h * HD:(h + 1) * HD, :] = dq_h[:, xx * TOK:(xx + 1) * TOK]
    for i in range(1, X):
        x_send(6, i, dq_send.at[lax.rem(x + i, X)], dq_recv)
    dq_recv[x] = dq_send[x]

    gsib.wait_recv()

    def g_copy(o):
        return rcopy(g_send.at[o], g_recv.at[o + 2], g_ss.at[o], g_rs.at[o + 2], ring_dev(o))

    def g_wait(o):
        slot = g_recv.at[o]
        rcopy(slot, slot, g_ss.at[0], g_rs.at[o], up).wait_recv()

    def g_term(zi):
        return gwp[core, zi].astype(F32) + g_sib[zi].astype(F32)

    def g_body(o, carry):
        zi = zmod(dest_off(o))
        g_send[o] = g_term(zi).astype(BF16)

        @pl.when(o >= 2)
        def _():
            g_wait(o)
            g_send[o] = (g_term(zi) + g_recv[o].astype(F32)).astype(BF16)

        g_copy(o).start()
        return carry

    lax.fori_loop(0, Z - 1, g_body, 0)

    for i in range(1, Y):
        y_recv(1, i, pj_recv)
    proj = pj_recv[0].astype(F32)
    for yy in range(1, Y):
        proj = proj + pj_recv[yy].astype(F32)
    proj_out[...] = proj.astype(BF16)
    for i in range(1, X):
        x_recv(6, i, dq_recv)
    for h in range(HEADS):
        dq_t = jnp.zeros((HD, TOK), F32)
        for xx in range(X):
            dq_t = dq_t + dq_recv[xx, h * HD:(h + 1) * HD, :].astype(F32)
        dq_out[:, h * HD:(h + 1) * HD] = dq_t.T.astype(BF16)
    last = Z - 1
    sib_copy(last).wait_recv()
    rs_wait(last)
    rs_wait(last + 1)
    for a, out in ((0, dk_out), (1, dv_out)):
        out[...] = (
            part[last, core, a].astype(F32)
            + sib_recv[last, a].astype(F32)
            + rs_recv[last, a].astype(F32)
            + rs_recv[last + 1, a].astype(F32)
        ).astype(BF16)
    g_wait(last)
    g_wait(last + 1)
    gw_out[...] = g_term(z) + g_recv[last].astype(F32) + g_recv[last + 1].astype(F32)

    for copy in sends:
        copy.wait_send()

    def drain(o, carry):
        sib_copy(o).wait_send()
        rs_copy(o).wait_send()
        g_copy(o).wait_send()
        return carry

    lax.fori_loop(0, Z - 1, drain, 0)
    sib_copy(last).wait_send()


def per_device(X, Z, Y, queries, key_rows, value_rows, out_weight, grad_projected, segment_len, block_order):
    gcols = grad_projected.shape[1]
    grow = out_weight.shape[0] // (X * Z * 2)
    QN = X * TOK
    vmem = pl.BlockSpec(memory_space=pltpu.VMEM)
    smem = pl.BlockSpec(memory_space=pltpu.SMEM)
    dma = pltpu.SemaphoreType.DMA
    scratch = [
        pltpu.VMEM((X, TOK, WID), BF16),
        pltpu.VMEM((X, TOK, WID), BF16),
        pltpu.VMEM((Z, 2, 2, TOK, WID), BF16),
        pltpu.VMEM((Y, TOK, gcols), BF16),
        pltpu.VMEM((X, TOK, gcols), BF16),
        pltpu.VMEM((Z, 2 * TOK, 128), jnp.int32),
        pltpu.VMEM((1, QN), jnp.int32),
        pltpu.VMEM((HEADS, Z, 2 * TOK, QN), F32),
        pltpu.VMEM((HEADS, Z, 2 * TOK, QN), F32),
        pltpu.VMEM((HEADS, Z, 1, QN), F32),
        pltpu.VMEM((HEADS, Z, 1, QN), F32),
        pltpu.VMEM((HEADS, Z, 1, QN), F32),
        pltpu.VMEM((HEADS, HD, QN), F32),
        pltpu.VMEM((HEADS, 1, QN), F32),
        pltpu.VMEM((8, QN), F32),
        pltpu.VMEM((X, 8, QN), F32),
        pltpu.VMEM((X, WID, TOK), BF16),
        pltpu.VMEM((X, WID, TOK), BF16),
        pltpu.VMEM((X, TOK, WID), BF16),
        pltpu.VMEM((HEADS, HD, QN), F32),
        pltpu.VMEM((X, WID, TOK), BF16),
        pltpu.VMEM((X, WID, TOK), BF16),
        pltpu.VMEM((Y, TOK, gcols), BF16),
        pltpu.VMEM((Y, TOK, gcols), BF16),
        pltpu.VMEM((HEADS, Z, 1, QN), F32),
        pltpu.VMEM((HEADS, 1, QN), F32),
        pltpu.VMEM((Z, 2, 2, TOK, WID), BF16),
        pltpu.VMEM((Z, 2, TOK, WID), BF16),
        pltpu.VMEM((Z, 2, TOK, WID), BF16),
        pltpu.VMEM((Z + 1, 2, TOK, WID), BF16),
        pltpu.VMEM((gcols, WID), F32),
        pltpu.VMEM((2, Z, grow, WID), BF16),
        pltpu.VMEM((Z, grow, WID), BF16),
        pltpu.VMEM((Z, grow, WID), BF16),
        pltpu.VMEM((Z + 1, grow, WID), BF16),
        dma((7, X)), dma((7, X)),
        dma((2, Y)), dma((2, Y)),
        dma((2, Z // 2, 2)), dma((2, Z // 2, 2)),
        dma((Z, 2)), dma((Z, 2)),
        dma((Z,)), dma((Z,)),
        dma((Z + 1,)), dma((Z + 1,)),
        dma, dma,
        dma((Z + 1,)), dma((Z + 1,)),
    ]
    out_shape = (
        jax.ShapeDtypeStruct((TOK, gcols), BF16),
        jax.ShapeDtypeStruct((TOK, WID), BF16),
        jax.ShapeDtypeStruct((TOK, WID), BF16),
        jax.ShapeDtypeStruct((TOK, WID), BF16),
        jax.ShapeDtypeStruct((grow, WID), F32),
    )
    return pl.pallas_call(
        functools.partial(kernel, X, Z, Y),
        out_shape=out_shape,
        in_specs=[smem, smem, vmem, vmem, vmem, vmem, vmem],
        out_specs=(vmem,) * 5,
        scratch_shapes=scratch,
        compiler_params=pltpu.CompilerParams(
            collective_id=0, has_side_effects=True, vmem_limit_bytes=60 * 1024 * 1024
        ),
        name="segment_attention",
    )(segment_len, block_order, queries, key_rows, value_rows, out_weight, grad_projected)


def solution(mesh):
    ctx = mesh.shape["ctx"]
    Y = mesh.shape["head"]
    X = Y
    Z = ctx // (2 * X)
    return jax.shard_map(
        functools.partial(per_device, X, Z, Y),
        mesh=mesh,
        in_specs=(
            P("ctx", "head"),
            P("ctx", "head"),
            P("ctx", "head"),
            P(None, "head"),
            P("ctx", "head"),
            P(),
            P(),
        ),
        out_specs=(P("ctx", "head"),) * 5,
        check_vma=False,
    )
```

```python
import functools
import math

import jax
import jax.numpy as jnp
from jax import lax
from jax.experimental import pallas as pl
from jax.experimental.pallas import tpu as pltpu
from jax.sharding import PartitionSpec as P

HD = 128
HEADS = 3
TOK = 128
WID = HEADS * HD
BLK = 64
SEGS = 8
SCALE = 1.0 / math.sqrt(HD)
EXP2_SCALE = SCALE * math.log2(math.e)
NEG_FILL = -1e30
MAX_FLOOR = -1e20
F32 = jnp.float32
BF16 = jnp.bfloat16
MESH = pl.DeviceIdType.MESH


def dot_nn(a, b):
    return jnp.dot(a, b, preferred_element_type=F32)


def dot_nt(a, b):
    return lax.dot_general(a, b, (((1,), (1,)), ((), ())), preferred_element_type=F32)


def dot_tn(a, b):
    return lax.dot_general(a, b, (((0,), (0,)), ((), ())), preferred_element_type=F32)


def head_lanes(h):
    return slice(h * HD, (h + 1) * HD)


def kernel(
    X, Z, Y,
    seg_len, order, q_in, k_in, v_in, w_hbm, gp_in,
    proj_out, dq_out, dk_out, dv_out, gw_out,
    qb, db, kvb, gpf, gpx, segk, segq, pbuf, dpbuf, mst, lst, dst,
    oacc, mrun, st_send, st_recv, sd_send, sd_recv, wbuf, o_send, o_recv, attb, dqacc, dq_send, dq_recv,
    pj_send, pj_recv, fac, delta, part, sib_recv, rs_send, rs_recv,
    gwf, gwp, g_sib, g_send, g_recv,
    w_sem,
    x_ss, x_rs, y_ss, y_rs, ring_ss, ring_rs, ksib_ss, ksib_rs,
    sib_ss, sib_rs, rs_ss, rs_rs, gsib_ss, gsib_rs, g_ss, g_rs,
):
    nplus, nminus = Z // 2, Z - 1 - Z // 2
    QN = X * TOK
    gcols = gp_in.shape[1]
    me = lax.axis_index("ctx")
    y = lax.axis_index("head")
    core = lax.rem(me, 2)
    z = lax.rem(me // 2, Z)
    x = me // (2 * Z)

    def ctx_of(xx, zz, cc):
        return (xx * Z + zz) * 2 + cc

    def zmod(off):
        return lax.rem(z + off + 2 * Z, Z)

    other = 1 - core
    sib = (ctx_of(x, z, other), y)
    up = (ctx_of(x, zmod(1), core), y)
    down = (ctx_of(x, zmod(-1), core), y)

    def x_dev(i):
        return (ctx_of(lax.rem(x + i, X), z, core), y)

    def y_dev(i):
        return (me, lax.rem(y + i, Y))

    def z_dev(i):
        return (ctx_of(x, zmod(i), core), y)

    def rcopy(src, dst_ref, ss, rs, dev):
        return pltpu.make_async_remote_copy(
            src_ref=src, dst_ref=dst_ref, send_sem=ss, recv_sem=rs,
            device_id=dev, device_id_type=MESH,
        )

    barrier = pltpu.get_barrier_semaphore()
    partners = [sib] + [z_dev(i) for i in range(1, Z)]
    partners += [x_dev(i) for i in range(1, X)] + [y_dev(i) for i in range(1, Y)]
    for dev in partners:
        pl.semaphore_signal(barrier, inc=1, device_id=dev, device_id_type=MESH)
    w_copy = pltpu.make_async_copy(w_hbm, wbuf, w_sem)
    w_copy.start()

    sends = []

    def go(copy):
        copy.start()
        sends.append(copy)

    def x_recv(kind, i, buf):
        slot = buf.at[lax.rem(x + X - i, X)]
        rcopy(slot, slot, x_ss.at[kind, i], x_rs.at[kind, i], x_dev(i)).wait_recv()

    def x_send(kind, i, src, buf):
        go(rcopy(src, buf.at[x], x_ss.at[kind, i], x_rs.at[kind, i], x_dev(i)))

    def y_recv(kind, i, buf):
        slot = buf.at[lax.rem(y + Y - i, Y)]
        rcopy(slot, slot, y_ss.at[kind, i], y_rs.at[kind, i], y_dev(i)).wait_recv()

    def y_send(kind, i, src, buf):
        go(rcopy(src, buf.at[y], y_ss.at[kind, i], y_rs.at[kind, i], y_dev(i)))

    half = TOK // 2

    def rows_of(hf):
        return pl.ds(hf * half, half)

    def x_half(kind, i, hf, src_dev):
        slot = db.at[src_dev, rows_of(hf)]
        return rcopy(slot, slot, x_ss.at[kind, i], x_rs.at[kind, i], x_dev(i))

    def y_half(hf, i, src, src_dev):
        slot = gpf.at[src_dev, rows_of(hf)]
        return rcopy(src, slot, y_ss.at[hf, i], y_rs.at[hf, i], y_dev(i))

    def kv_slot(off, cc, a):
        return kvb.at[zmod(off), cc, a]

    def limit(direction, a):
        return nplus if direction == a else nminus

    def ring_send(direction, step, a, src):
        off = 1 - step if direction == 0 else step - 1
        go(rcopy(
            src, kv_slot(off, core, a),
            ring_ss.at[direction, step - 1, a], ring_rs.at[direction, step - 1, a],
            up if direction == 0 else down,
        ))

    def ring_wait(direction, step, a):
        off = -step if direction == 0 else step
        slot = kv_slot(off, core, a)
        rcopy(
            slot, slot, ring_ss.at[direction, step - 1, a],
            ring_rs.at[direction, step - 1, a], up,
        ).wait_recv()

    def sib_index(off):
        return nplus + off if off > 0 else -off

    def ksib_send(off, a, src):
        j = sib_index(off)
        go(rcopy(src, kv_slot(off, core, a), ksib_ss.at[j, a], ksib_rs.at[j, a], sib))

    def ksib_wait(off, a):
        j = sib_index(off)
        slot = kv_slot(off, other, a)
        rcopy(slot, slot, ksib_ss.at[j, a], ksib_rs.at[j, a], sib).wait_recv()

    ends = []
    total = seg_len[0]
    for i in range(SEGS - 1):
        ends.append(total)
        total = total + seg_len[i + 1]

    def segments(row_in_block, ctx_id):
        first = order[2 * ctx_id] * BLK
        second = order[2 * ctx_id + 1] * BLK - BLK
        pos = row_in_block + jnp.where(row_in_block < BLK, first, second)
        seg = jnp.zeros_like(pos)
        for end in ends:
            seg = seg + jnp.where(pos >= end, 1, 0)
        return seg

    lanes = lax.broadcasted_iota(jnp.int32, (1, TOK), 1)
    for xx in range(X):
        segq[:, xx * TOK:(xx + 1) * TOK] = segments(lanes, ctx_of(xx, z, core))
    rows = lax.broadcasted_iota(jnp.int32, (TOK, 128), 0)

    def seg_body(zz, carry):
        for cc in range(2):
            segk[zz, cc * TOK:(cc + 1) * TOK, :] = segments(rows, ctx_of(x, zz, cc))
        return carry

    lax.fori_loop(0, Z, seg_body, 0)
    for h in range(HEADS):
        mrun[h] = jnp.full((1, QN), MAX_FLOOR, F32)
        oacc[h] = jnp.zeros((HD, QN), F32)
        dqacc[h] = jnp.zeros((HD, QN), F32)

    qb[x] = q_in[...]
    kvb[z, core, 0] = k_in[...]
    kvb[z, core, 1] = v_in[...]
    gpf[y] = gp_in[...]
    pl.semaphore_wait(barrier, len(partners))

    def send_gp(hf):
        for i in range(1, Y):
            go(y_half(hf, i, gp_in.at[rows_of(hf)], y))

    send_gp(0)
    for a, src in ((0, k_in), (1, v_in)):
        for direction in range(2):
            if limit(direction, a) >= 1:
                ring_send(direction, 1, a, src)
        ksib_send(0, a, src)
    for i in range(1, X):
        x_send(0, i, q_in, qb)
    send_gp(1)

    def keys(zi, a, h):
        return kvb[zi, :, a, :, head_lanes(h)].reshape(2 * TOK, HD)

    def gathered(buf, h):
        return buf[:, :, head_lanes(h)].reshape(QN, HD)

    def fwd(zi):
        def body(h):
            s = dot_nt(keys(zi, 0, h), gathered(qb, h))
            sk = jnp.concatenate([segk[zi]] * X, axis=1)
            s = jnp.where(sk <= segq[...], s, NEG_FILL)
            m = jnp.maximum(jnp.max(s, axis=0, keepdims=True), MAX_FLOOR)
            p = jnp.exp2((s - m) * EXP2_SCALE)
            pbuf[h, zi] = p
            mst[h, zi] = m
            lst[h, zi] = jnp.sum(p, axis=0, keepdims=True)
            pv = dot_tn(keys(zi, 1, h), p.astype(BF16))
            m_old = mrun[h]
            m_new = jnp.maximum(m_old, m)
            mrun[h] = m_new
            oacc[h] = (
                oacc[h] * jnp.exp2((m_old - m_new) * EXP2_SCALE)
                + pv * jnp.exp2((m - m_new) * EXP2_SCALE)
            )

        for h in range(HEADS):
            body(h)

    def dprob(zi):
        def body(h):
            dp = dot_nt(keys(zi, 1, h), gathered(db, h))
            dpbuf[h, zi] = dp
            dst[h, zi] = jnp.sum(dp * pbuf[h, zi], axis=0, keepdims=True)

        for h in range(HEADS):
            body(h)

    def ring_step(step):
        for a in range(2):
            for direction in range(2):
                off = -step if direction == 0 else step
                far = limit(direction, a)
                if step <= far:
                    ring_wait(direction, step, a)
                    if step < far:
                        ring_send(direction, step + 1, a, kv_slot(off, core, a))
                    ksib_send(-step if step == nplus else off, a, kv_slot(off, core, a))

    def step_offsets(step):
        return [0] if step == 0 else ([-step, step] if step <= nminus else [-step])

    def sib_ready(step):
        for off in step_offsets(step):
            for a in range(2):
                ksib_wait(off, a)

    def over(step, fn):
        offs = step_offsets(step)
        if len(offs) == 1:
            fn(zmod(offs[0]))
        else:
            def body(i, carry):
                fn(zmod(step * (2 * i - 1)))
                return carry

            lax.fori_loop(0, 2, body, 0)

    def dout_half(hf):
        acc = None
        for i in range(Y):
            src_y = lax.rem(y + Y - i, Y)
            if i:
                y_half(hf, i, gpf.at[src_y, rows_of(hf)], src_y).wait_recv()
            w_rows = wbuf[pl.ds(pl.multiple_of(src_y * gcols, gcols), gcols), :]
            term = dot_nn(gpf[src_y, rows_of(hf), :], w_rows)
            acc = term if acc is None else acc + term
        db[x, rows_of(hf), :] = acc.astype(BF16)
        for i in range(1, X):
            go(x_half(1 + hf, i, hf, x))

    w_copy.wait()
    ring_step(1)
    for i in range(1, X):
        x_recv(0, i, qb)
    sib_ready(0)
    over(0, fwd)
    dout_half(0)
    ring_step(2)
    sib_ready(1)
    over(1, fwd)
    dout_half(1)
    ring_step(3)
    sib_ready(2)
    over(2, fwd)
    sib_ready(3)
    over(3, fwd)
    ring_step(4)
    for hf in range(2):
        for i in range(1, X):
            x_half(1 + hf, i, hf, lax.rem(x + X - i, X)).wait_recv()
    for step in range(3):
        over(step, dprob)
    sib_ready(4)
    over(4, fwd)

    inverse, part_w = [], []
    for h in range(HEADS):
        m_top = mrun[h]
        w = jnp.exp2((mst[h] - m_top[None]) * EXP2_SCALE)
        l_sum = jnp.maximum(jnp.sum(lst[h] * w, axis=0), 1e-30)
        inv = 1.0 / l_sum
        part_w.append(w)
        inverse.append(inv)
        st_send[h:h + 1, :] = m_top * EXP2_SCALE + jnp.log2(l_sum)
        o_h = (oacc[h] * inv).astype(BF16)
        for xx in range(X):
            o_send[xx, h * HD:(h + 1) * HD, :] = o_h[:, xx * TOK:(xx + 1) * TOK]
    st_send[HEADS:8, :] = jnp.zeros((8 - HEADS, QN), F32)
    for i in range(1, X):
        x_send(4, i, st_send, st_recv)
    for i in range(1, X):
        x_send(5, i, o_send.at[lax.rem(x + i, X)], o_recv)
    for step in range(3, nplus + 1):
        over(step, dprob)
    for h in range(HEADS):
        sd_send[h:h + 1, :] = jnp.sum(dst[h] * part_w[h], axis=0) * inverse[h]
    sd_send[HEADS:8, :] = jnp.zeros((8 - HEADS, QN), F32)
    for i in range(1, X):
        x_send(6, i, sd_send, sd_recv)
    for i in range(1, X):
        x_send(3, i, gpf.at[lax.rem(x + i, X)], gpx)
    gpx[x] = gpf[x]
    st_recv[x] = st_send[...]
    o_recv[x] = o_send[x]
    sd_recv[x] = sd_send[...]
    for i in range(1, X):
        x_recv(4, i, st_recv)
    lse_all = st_recv[:, 0:HEADS, :]
    top = jnp.max(lse_all, axis=0)
    lse = top + jnp.log2(jnp.sum(jnp.exp2(lse_all - top[None]), axis=0))
    weight = jnp.exp2(lse_all - lse[None])
    for h in range(HEADS):
        fac[h] = jnp.exp2(mst[h] * EXP2_SCALE - lse[h:h + 1][None])
    for i in range(1, X):
        x_recv(6, i, sd_recv)
    delta_all = jnp.sum(weight * sd_recv[:, 0:HEADS, :], axis=0)
    for h in range(HEADS):
        delta[h] = delta_all[h:h + 1]
    own_stats = st_recv[:, 0:HEADS, pl.ds(pl.multiple_of(x * TOK, TOK), TOK)]
    own_top = jnp.max(own_stats, axis=0)
    own_w = jnp.exp2(own_stats - own_top[None])
    own_w = own_w / jnp.sum(own_w, axis=0)[None]

    def dest_off(o):
        pair = o // 2
        return jnp.where(lax.rem(o, 2) == 0, nplus - pair, pair - nminus)

    def bwd(o):
        zi = zmod(dest_off(o))

        def body(h):
            lanes_h = head_lanes(h)
            p = pbuf[h, zi] * fac[h, zi]
            ds = (p * (dpbuf[h, zi] - delta[h])).astype(BF16)
            dv = dot_nn(p.astype(BF16), gathered(db, h)).astype(BF16)
            dk = (dot_nn(ds, gathered(qb, h)) * SCALE).astype(BF16)
            for cc in range(2):
                part[o, cc, 0, :, lanes_h] = dk[cc * TOK:(cc + 1) * TOK]
                part[o, cc, 1, :, lanes_h] = dv[cc * TOK:(cc + 1) * TOK]
            dqacc[h] = dqacc[h] + dot_tn(keys(zi, 0, h), ds)

        for h in range(HEADS):
            body(h)

    def sib_copy(o, a):
        return rcopy(
            part.at[o, other, a], sib_recv.at[o, a], sib_ss.at[o, a], sib_rs.at[o, a], sib
        )

    def rs_copy(o, a):
        if a == 0:
            slot = o + 2
            off = jnp.where(lax.rem(o, 2) == 0, 1, -1)
        else:
            slot = jnp.where(o == 0, 1, o + 2)
            off = jnp.where((lax.rem(o, 2) == 0) & (o > 0), 1, -1)
        return rcopy(
            rs_send.at[o, a], rs_recv.at[slot, a], rs_ss.at[o, a], rs_rs.at[slot, a], z_dev(off)
        )

    def rs_wait(o, a):
        slot = rs_recv.at[o, a]
        rcopy(slot, slot, rs_ss.at[0, a], rs_rs.at[o, a], up).wait_recv()

    def finalize(o, a):
        sib_copy(o, a).wait_recv()
        total = part[o, core, a].astype(F32) + sib_recv[o, a].astype(F32)
        if o >= 2 + a or (a == 1 and o == 1):
            rs_wait(o, a)
            total = total + rs_recv[o, a].astype(F32)
        rs_send[o, a] = total.astype(BF16)
        rs_copy(o, a).start()

    def bwd_range(first, last):
        def body(o, carry):
            bwd(o)
            for a in range(2):
                sib_copy(o, a).start()
            return carry

        lax.fori_loop(first, last, body, 0)

    bwd_range(0, 2)
    finalize(0, 0)
    finalize(0, 1)
    finalize(1, 0)

    for i in range(1, X):
        x_recv(5, i, o_recv)
    for h in range(HEADS):
        o_t = jnp.zeros((HD, TOK), F32)
        for xx in range(X):
            o_t = o_t + o_recv[xx, h * HD:(h + 1) * HD, :].astype(F32) * own_w[xx, h:h + 1]
        attb[x, :, h * HD:(h + 1) * HD] = o_t.T.astype(BF16)
    for i in range(1, X):
        x_send(7, i, attb.at[x], attb)
    bwd_range(2, 5)
    finalize(2, 1)
    finalize(1, 1)
    finalize(2, 0)
    bwd_range(5, Z)

    for h in range(HEADS):
        dq_h = (dqacc[h] * SCALE).astype(BF16)
        for xx in range(X):
            dq_send[xx, h * HD:(h + 1) * HD, :] = dq_h[:, xx * TOK:(xx + 1) * TOK]
    for i in range(1, X):
        x_send(8, i, dq_send.at[lax.rem(x + i, X)], dq_recv)
    dq_recv[x] = dq_send[x]

    att = attb[x]
    for i in range(1, Y):
        dst_y = lax.rem(y + i, Y)
        w_rows = wbuf[pl.ds(pl.multiple_of(dst_y * gcols, gcols), gcols), :]
        pj_send[dst_y] = dot_nt(att, w_rows).astype(BF16)
        y_send(2, i, pj_send.at[dst_y], pj_recv)
    w_rows = wbuf[pl.ds(pl.multiple_of(y * gcols, gcols), gcols), :]
    pj_recv[y] = dot_nt(att, w_rows).astype(BF16)
    for o in (3, 4):
        for a in range(2):
            finalize(o, a)

    for i in range(1, X):
        x_recv(3, i, gpx)
    for i in range(1, X):
        x_recv(7, i, attb)
    att_all = attb[...].reshape(QN, WID)

    def gw_body(j, carry):
        lanes_j = pl.ds(pl.multiple_of(j * 128, 128), 128)
        left = gpx[:, :, lanes_j].reshape(QN, 128)
        gwf[pl.ds(pl.multiple_of(j * 128, 128), 128), :] = dot_tn(left, att_all)
        return carry

    lax.fori_loop(0, gcols // 128, gw_body, 0)
    grow = gw_out.shape[0]
    for zz in range(Z):
        for cc in range(2):
            first = (zz * 2 + cc) * grow
            gwp[cc, zz] = gwf[first:first + grow, :].astype(BF16)
    gsib = rcopy(gwp.at[other], g_sib, gsib_ss, gsib_rs, sib)
    go(gsib)

    for a in range(2):
        finalize(5, a)
    gsib.wait_recv()
    for i in range(1, Z):
        zi = zmod(i)
        g_send[i] = (gwp[core, zi].astype(F32) + g_sib[zi].astype(F32)).astype(BF16)
        go(rcopy(g_send.at[i], g_recv.at[i], g_ss.at[i], g_rs.at[i], z_dev(i)))
    for a in range(2):
        finalize(6, a)

    for i in range(1, Y):
        y_recv(2, i, pj_recv)
    proj = pj_recv[0].astype(F32)
    for yy in range(1, Y):
        proj = proj + pj_recv[yy].astype(F32)
    proj_out[...] = proj.astype(BF16)
    for i in range(1, X):
        x_recv(8, i, dq_recv)
    for h in range(HEADS):
        dq_t = jnp.zeros((HD, TOK), F32)
        for xx in range(X):
            dq_t = dq_t + dq_recv[xx, h * HD:(h + 1) * HD, :].astype(F32)
        dq_out[:, h * HD:(h + 1) * HD] = dq_t.T.astype(BF16)
    g_total = gwp[core, z].astype(F32) + g_sib[z].astype(F32)
    for i in range(1, Z):
        rcopy(g_recv.at[i], g_recv.at[i], g_ss.at[i], g_rs.at[i], z_dev(i)).wait_recv()
        g_total = g_total + g_recv[i].astype(F32)
    gw_out[...] = g_total
    last = Z - 1
    for a, out in ((0, dk_out), (1, dv_out)):
        sib_copy(last, a).wait_recv()
        rs_wait(last, a)
        rs_wait(last + 1, a)
        out[...] = (
            part[last, core, a].astype(F32)
            + sib_recv[last, a].astype(F32)
            + rs_recv[last, a].astype(F32)
            + rs_recv[last + 1, a].astype(F32)
        ).astype(BF16)

    for copy in sends:
        copy.wait_send()
    for a in range(2):
        for o in range(Z):
            sib_copy(o, a).wait_send()
            if o < last:
                rs_copy(o, a).wait_send()


def finish(*refs):
    half = len(refs) // 2
    for src, out in zip(refs[:half], refs[half:]):
        out[...] = src[...]


def per_device(X, Z, Y, queries, key_rows, value_rows, out_weight, grad_projected, segment_len, block_order):
    gcols = grad_projected.shape[1]
    grow = out_weight.shape[0] // (X * Z * 2)
    QN = X * TOK
    vmem = pl.BlockSpec(memory_space=pltpu.VMEM)
    smem = pl.BlockSpec(memory_space=pltpu.SMEM)
    dma = pltpu.SemaphoreType.DMA
    scratch = [
        pltpu.VMEM((X, TOK, WID), BF16),
        pltpu.VMEM((X, TOK, WID), BF16),
        pltpu.VMEM((Z, 2, 2, TOK, WID), BF16),
        pltpu.VMEM((Y, TOK, gcols), BF16),
        pltpu.VMEM((X, TOK, gcols), BF16),
        pltpu.VMEM((Z, 2 * TOK, 128), jnp.int32),
        pltpu.VMEM((1, QN), jnp.int32),
        pltpu.VMEM((HEADS, Z, 2 * TOK, QN), F32),
        pltpu.VMEM((HEADS, Z, 2 * TOK, QN), F32),
        pltpu.VMEM((HEADS, Z, 1, QN), F32),
        pltpu.VMEM((HEADS, Z, 1, QN), F32),
        pltpu.VMEM((HEADS, Z, 1, QN), F32),
        pltpu.VMEM((HEADS, HD, QN), F32),
        pltpu.VMEM((HEADS, 1, QN), F32),
        pltpu.VMEM((8, QN), F32),
        pltpu.VMEM((X, 8, QN), F32),
        pltpu.VMEM((8, QN), F32),
        pltpu.VMEM((X, 8, QN), F32),
        pltpu.VMEM(out_weight.shape, BF16),
        pltpu.VMEM((X, WID, TOK), BF16),
        pltpu.VMEM((X, WID, TOK), BF16),
        pltpu.VMEM((X, TOK, WID), BF16),
        pltpu.VMEM((HEADS, HD, QN), F32),
        pltpu.VMEM((X, WID, TOK), BF16),
        pltpu.VMEM((X, WID, TOK), BF16),
        pltpu.VMEM((Y, TOK, gcols), BF16),
        pltpu.VMEM((Y, TOK, gcols), BF16),
        pltpu.VMEM((HEADS, Z, 1, QN), F32),
        pltpu.VMEM((HEADS, 1, QN), F32),
        pltpu.VMEM((Z, 2, 2, TOK, WID), BF16),
        pltpu.VMEM((Z, 2, TOK, WID), BF16),
        pltpu.VMEM((Z, 2, TOK, WID), BF16),
        pltpu.VMEM((Z + 1, 2, TOK, WID), BF16),
        pltpu.VMEM((gcols, WID), F32),
        pltpu.VMEM((2, Z, grow, WID), BF16),
        pltpu.VMEM((Z, grow, WID), BF16),
        pltpu.VMEM((Z, grow, WID), BF16),
        pltpu.VMEM((Z, grow, WID), BF16),
        dma,
        dma((9, X)), dma((9, X)),
        dma((3, Y)), dma((3, Y)),
        dma((2, Z // 2, 2)), dma((2, Z // 2, 2)),
        dma((Z, 2)), dma((Z, 2)),
        dma((Z, 2)), dma((Z, 2)),
        dma((Z + 1, 2)), dma((Z + 1, 2)),
        dma, dma,
        dma((Z,)), dma((Z,)),
    ]
    out_shape = (
        jax.ShapeDtypeStruct((TOK, gcols), BF16),
        jax.ShapeDtypeStruct((TOK, WID), BF16),
        jax.ShapeDtypeStruct((TOK, WID), BF16),
        jax.ShapeDtypeStruct((TOK, WID), BF16),
        jax.ShapeDtypeStruct((grow, WID), F32),
    )
    results = pl.pallas_call(
        functools.partial(kernel, X, Z, Y),
        out_shape=out_shape,
        in_specs=[smem, smem, vmem, vmem, vmem, pl.BlockSpec(memory_space=pl.ANY), vmem],
        out_specs=(vmem,) * 5,
        scratch_shapes=scratch,
        compiler_params=pltpu.CompilerParams(
            collective_id=0, has_side_effects=True, vmem_limit_bytes=60 * 1024 * 1024
        ),
        name="segment_attention",
    )(segment_len, block_order, queries, key_rows, value_rows, out_weight, grad_projected)
    return pl.pallas_call(
        finish,
        out_shape=out_shape,
        in_specs=[vmem] * 5,
        out_specs=(vmem,) * 5,
        name="outputs",
    )(*results)


def solution(mesh):
    ctx = mesh.shape["ctx"]
    Y = mesh.shape["head"]
    X = Y
    Z = ctx // (2 * X)
    return jax.shard_map(
        functools.partial(per_device, X, Z, Y),
        mesh=mesh,
        in_specs=(
            P("ctx", "head"),
            P("ctx", "head"),
            P("ctx", "head"),
            P(None, "head"),
            P("ctx", "head"),
            P(),
            P(),
        ),
        out_specs=(P("ctx", "head"),) * 5,
        check_vma=False,
    )
```

```python
import functools
import math

import jax
import jax.numpy as jnp
from jax import lax
from jax.experimental import pallas as pl
from jax.experimental.pallas import tpu as pltpu
from jax.sharding import PartitionSpec as P

HD = 128
HEADS = 3
TOK = 128
WID = HEADS * HD
BLK = 64
SEGS = 8
SCALE = 1.0 / math.sqrt(HD)
EXP2_SCALE = SCALE * math.log2(math.e)
NEG_FILL = -1e30
MAX_FLOOR = -1e20
F32 = jnp.float32
BF16 = jnp.bfloat16
MESH = pl.DeviceIdType.MESH


def dot_nn(a, b):
    return jnp.dot(a, b, preferred_element_type=F32)


def dot_nt(a, b):
    return lax.dot_general(a, b, (((1,), (1,)), ((), ())), preferred_element_type=F32)


def dot_tn(a, b):
    return lax.dot_general(a, b, (((0,), (0,)), ((), ())), preferred_element_type=F32)


def head_lanes(h):
    return slice(h * HD, (h + 1) * HD)


def kernel(
    X, Z, Y,
    seg_len, order, q_in, k_in, v_in, w_hbm, gp_in,
    proj_out, dq_out, dk_out, dv_out, gw_out,
    qb, db, kvb, gpf, gpx, segk, segq, pbuf, dpbuf, mst, lst, dst,
    oacc, mrun, st_send, st_recv, wbuf, o_send, o_recv, attb, dqacc, dq_send, dq_recv,
    pj_send, pj_recv, fac, delta, part, sib_recv, rs_send, rs_recv,
    gwf, gwp, g_sib, g_send, g_recv,
    w_sem,
    x_ss, x_rs, gx_ss, gx_rs, y_ss, y_rs, ring_ss, ring_rs, ksib_ss, ksib_rs,
    sib_ss, sib_rs, rs_ss, rs_rs, gsib_ss, gsib_rs, g_ss, g_rs,
):
    nplus, nminus = Z // 2, Z - 1 - Z // 2
    QN = X * TOK
    gcols = gp_in.shape[1]
    me = lax.axis_index("ctx")
    y = lax.axis_index("head")
    core = lax.rem(me, 2)
    z = lax.rem(me // 2, Z)
    x = me // (2 * Z)

    def ctx_of(xx, zz, cc):
        return (xx * Z + zz) * 2 + cc

    def zmod(off):
        return lax.rem(z + off + 2 * Z, Z)

    other = 1 - core
    sib = (ctx_of(x, z, other), y)
    up = (ctx_of(x, zmod(1), core), y)
    down = (ctx_of(x, zmod(-1), core), y)

    def x_dev(i):
        return (ctx_of(lax.rem(x + i, X), z, core), y)

    def y_dev(i):
        return (me, lax.rem(y + i, Y))

    def z_dev(i):
        return (ctx_of(x, zmod(i), core), y)

    def rcopy(src, dst_ref, ss, rs, dev):
        return pltpu.make_async_remote_copy(
            src_ref=src, dst_ref=dst_ref, send_sem=ss, recv_sem=rs,
            device_id=dev, device_id_type=MESH,
        )

    barrier = pltpu.get_barrier_semaphore()
    partners = [sib] + [z_dev(i) for i in (1, -1, 2, -2)]
    partners += [x_dev(i) for i in range(1, X)] + [y_dev(i) for i in range(1, Y)]
    for dev in partners:
        pl.semaphore_signal(barrier, inc=1, device_id=dev, device_id_type=MESH)
    w_copy = pltpu.make_async_copy(w_hbm, wbuf, w_sem)
    w_copy.start()

    sends = []

    def go(copy):
        copy.start()
        sends.append(copy)

    def x_recv(kind, i, buf):
        slot = buf.at[lax.rem(x + X - i, X)]
        rcopy(slot, slot, x_ss.at[kind, i], x_rs.at[kind, i], x_dev(i)).wait_recv()

    def x_send(kind, i, src, buf):
        go(rcopy(src, buf.at[x], x_ss.at[kind, i], x_rs.at[kind, i], x_dev(i)))

    def y_recv(kind, i, buf):
        slot = buf.at[lax.rem(y + Y - i, Y)]
        rcopy(slot, slot, y_ss.at[kind, i], y_rs.at[kind, i], y_dev(i)).wait_recv()

    def y_send(kind, i, src, buf):
        go(rcopy(src, buf.at[y], y_ss.at[kind, i], y_rs.at[kind, i], y_dev(i)))

    half = TOK // 2

    def rows_of(hf):
        return pl.ds(hf * half, half)

    def x_half(kind, i, hf, src_dev):
        slot = db.at[src_dev, rows_of(hf)]
        return rcopy(slot, slot, x_ss.at[kind, i], x_rs.at[kind, i], x_dev(i))

    def gx_half(i, hf, src, src_dev):
        slot = gpx.at[src_dev, rows_of(hf)]
        src = slot if src is None else src
        return rcopy(src, slot, gx_ss.at[i, hf], gx_rs.at[i, hf], x_dev(i))

    def o_piece(i, h, src_dev, dst_dev):
        rows_h = pl.ds(h * HD, HD)
        return rcopy(
            o_send.at[dst_dev, rows_h], o_recv.at[src_dev, rows_h],
            x_ss.at[5 + h, i], x_rs.at[5 + h, i], x_dev(i),
        )

    def att_piece(i, h, src_dev):
        slot = attb.at[src_dev, h]
        return rcopy(slot, slot, x_ss.at[8 + h, i], x_rs.at[8 + h, i], x_dev(i))

    def y_half(hf, i, src, src_dev):
        slot = gpf.at[src_dev, rows_of(hf)]
        return rcopy(src, slot, y_ss.at[hf, i], y_rs.at[hf, i], y_dev(i))

    def kv_slot(off, cc, a):
        return kvb.at[zmod(off), cc, a]

    def limit(direction, a):
        return nplus if direction == a else nminus

    def ring_send(direction, step, a, src):
        off = 1 - step if direction == 0 else step - 1
        go(rcopy(
            src, kv_slot(off, core, a),
            ring_ss.at[direction, step - 1, a], ring_rs.at[direction, step - 1, a],
            up if direction == 0 else down,
        ))

    def ring_wait(direction, step, a):
        off = -step if direction == 0 else step
        slot = kv_slot(off, core, a)
        rcopy(
            slot, slot, ring_ss.at[direction, step - 1, a],
            ring_rs.at[direction, step - 1, a], up,
        ).wait_recv()

    def sib_index(off):
        return nplus + off if off > 0 else -off

    def ksib_send(off, a, src):
        j = sib_index(off)
        go(rcopy(src, kv_slot(off, core, a), ksib_ss.at[j, a], ksib_rs.at[j, a], sib))

    def ksib_wait(off, a):
        j = sib_index(off)
        slot = kv_slot(off, other, a)
        rcopy(slot, slot, ksib_ss.at[j, a], ksib_rs.at[j, a], sib).wait_recv()

    ends = []
    total = seg_len[0]
    for i in range(SEGS - 1):
        ends.append(total)
        total = total + seg_len[i + 1]

    def segments(row_in_block, ctx_id):
        first = order[2 * ctx_id] * BLK
        second = order[2 * ctx_id + 1] * BLK - BLK
        pos = row_in_block + jnp.where(row_in_block < BLK, first, second)
        seg = jnp.zeros_like(pos)
        for end in ends:
            seg = seg + jnp.where(pos >= end, 1, 0)
        return seg

    lanes = lax.broadcasted_iota(jnp.int32, (1, TOK), 1)
    for xx in range(X):
        segq[:, xx * TOK:(xx + 1) * TOK] = segments(lanes, ctx_of(xx, z, core))
    rows = lax.broadcasted_iota(jnp.int32, (TOK, 128), 0)

    def seg_body(zz, carry):
        for cc in range(2):
            segk[zz, cc * TOK:(cc + 1) * TOK, :] = segments(rows, ctx_of(x, zz, cc))
        return carry

    lax.fori_loop(0, Z, seg_body, 0)
    for h in range(HEADS):
        mrun[h] = jnp.full((1, QN), MAX_FLOOR, F32)
        oacc[h] = jnp.zeros((HD, QN), F32)
        dqacc[h] = jnp.zeros((HD, QN), F32)

    qb[x] = q_in[...]
    kvb[z, core, 0] = k_in[...]
    kvb[z, core, 1] = v_in[...]
    gpf[y] = gp_in[...]
    pl.semaphore_wait(barrier, len(partners))

    def send_gp(hf):
        for i in range(1, Y):
            go(y_half(hf, i, gp_in.at[rows_of(hf)], y))

    send_gp(0)
    for turn in range(2):
        for direction in range(2):
            a = (direction + turn) % 2
            ring_send(direction, 1, a, (k_in, v_in)[a])
    for a in range(2):
        ksib_send(0, a, (k_in, v_in)[a])
    for i in range(1, X):
        x_send(0, i, q_in, qb)
    send_gp(1)

    def keys(zi, a, h):
        return kvb[zi, :, a, :, head_lanes(h)].reshape(2 * TOK, HD)

    def gathered(buf, h):
        return buf[:, :, head_lanes(h)].reshape(QN, HD)

    def fwd(zi):
        def body(h):
            s = dot_nt(keys(zi, 0, h), gathered(qb, h))
            sk = jnp.concatenate([segk[zi]] * X, axis=1)
            s = jnp.where(sk <= segq[...], s, NEG_FILL)
            m = jnp.maximum(jnp.max(s, axis=0, keepdims=True), MAX_FLOOR)
            p = jnp.exp2((s - m) * EXP2_SCALE)
            pbuf[h, zi] = p
            mst[h, zi] = m
            lst[h, zi] = jnp.sum(p, axis=0, keepdims=True)
            pv = dot_tn(keys(zi, 1, h), p.astype(BF16))
            m_old = mrun[h]
            m_new = jnp.maximum(m_old, m)
            mrun[h] = m_new
            oacc[h] = (
                oacc[h] * jnp.exp2((m_old - m_new) * EXP2_SCALE)
                + pv * jnp.exp2((m - m_new) * EXP2_SCALE)
            )

        for h in range(HEADS):
            body(h)

    def dprob(zi):
        def body(h):
            dp = dot_nt(keys(zi, 1, h), gathered(db, h))
            dpbuf[h, zi] = dp
            dst[h, zi] = jnp.sum(dp * pbuf[h, zi], axis=0, keepdims=True)

        for h in range(HEADS):
            body(h)

    def ring_step(step):
        for turn in range(2):
            for direction in range(2):
                a = (direction + turn) % 2
                off = -step if direction == 0 else step
                far = limit(direction, a)
                if step <= far:
                    ring_wait(direction, step, a)
                    if step < far:
                        ring_send(direction, step + 1, a, kv_slot(off, core, a))
                    ksib_send(-step if step == nplus else off, a, kv_slot(off, core, a))

    def step_offsets(step):
        return [0] if step == 0 else ([-step, step] if step <= nminus else [-step])

    def sib_ready(step):
        for off in step_offsets(step):
            for a in range(2):
                ksib_wait(off, a)

    def over(step, fn):
        offs = step_offsets(step)
        if len(offs) == 1:
            fn(zmod(offs[0]))
        else:
            def body(i, carry):
                fn(zmod(step * (2 * i - 1)))
                return carry

            lax.fori_loop(0, 2, body, 0)

    def dout_half(hf):
        acc = None
        for i in range(Y):
            src_y = lax.rem(y + Y - i, Y)
            if i:
                y_half(hf, i, gpf.at[src_y, rows_of(hf)], src_y).wait_recv()
            w_rows = wbuf[pl.ds(pl.multiple_of(src_y * gcols, gcols), gcols), :]
            term = dot_nn(gpf[src_y, rows_of(hf), :], w_rows)
            acc = term if acc is None else acc + term
        db[x, rows_of(hf), :] = acc.astype(BF16)
        for i in range(1, X):
            go(x_half(1 + hf, i, hf, x))
        for i in range(1, X):
            go(gx_half(i, hf, gpf.at[lax.rem(x + i, X), rows_of(hf)], x))
        gpx[x, rows_of(hf), :] = gpf[x, rows_of(hf), :]

    w_copy.wait()
    ring_step(1)
    for i in range(1, X):
        x_recv(0, i, qb)
    sib_ready(0)
    over(0, fwd)
    dout_half(0)
    ring_step(2)
    sib_ready(1)
    over(1, fwd)
    dout_half(1)
    ring_step(3)
    sib_ready(2)
    over(2, fwd)
    sib_ready(3)
    over(3, fwd)
    for hf in range(2):
        for i in range(1, X):
            x_half(1 + hf, i, hf, lax.rem(x + X - i, X)).wait_recv()
    for step in range(2):
        over(step, dprob)
    ring_step(4)
    for step in range(2, 4):
        over(step, dprob)
    sib_ready(4)
    over(4, fwd)
    over(4, dprob)

    inverse = []
    for h in range(HEADS):
        m_top = mrun[h]
        w = jnp.exp2((mst[h] - m_top[None]) * EXP2_SCALE)
        l_sum = jnp.maximum(jnp.sum(lst[h] * w, axis=0), 1e-30)
        inv = 1.0 / l_sum
        inverse.append(inv)
        st_send[h:h + 1, :] = m_top * EXP2_SCALE + jnp.log2(l_sum)
        st_send[HEADS + h:HEADS + h + 1, :] = jnp.sum(dst[h] * w, axis=0) * inv
    st_send[2 * HEADS:8, :] = jnp.zeros((8 - 2 * HEADS, QN), F32)
    for i in range(1, X):
        x_send(3, i, st_send, st_recv)
    for h in range(HEADS):
        o_h = (oacc[h] * inverse[h]).astype(BF16)
        for xx in range(X):
            o_send[xx, h * HD:(h + 1) * HD, :] = o_h[:, xx * TOK:(xx + 1) * TOK]
        for i in range(1, X):
            go(o_piece(i, h, x, lax.rem(x + i, X)))
    st_recv[x] = st_send[...]
    o_recv[x] = o_send[x]
    for i in range(1, X):
        x_recv(3, i, st_recv)
    lse_all = st_recv[:, 0:HEADS, :]
    top = jnp.max(lse_all, axis=0)
    lse = top + jnp.log2(jnp.sum(jnp.exp2(lse_all - top[None]), axis=0))
    weight = jnp.exp2(lse_all - lse[None])
    for h in range(HEADS):
        fac[h] = jnp.exp2(mst[h] * EXP2_SCALE - lse[h:h + 1][None])
    delta_all = jnp.sum(weight * st_recv[:, HEADS:2 * HEADS, :], axis=0)
    for h in range(HEADS):
        delta[h] = delta_all[h:h + 1]
    def dest_off(o):
        pair = o // 2
        return jnp.where(lax.rem(o, 2) == 0, nplus - pair, pair - nminus)

    def bwd(o):
        zi = zmod(dest_off(o))

        def body(h):
            lanes_h = head_lanes(h)
            p = pbuf[h, zi] * fac[h, zi]
            ds = (p * (dpbuf[h, zi] - delta[h])).astype(BF16)
            dv = dot_nn(p.astype(BF16), gathered(db, h)).astype(BF16)
            dk = (dot_nn(ds, gathered(qb, h)) * SCALE).astype(BF16)
            for cc in range(2):
                part[o, cc, 0, :, lanes_h] = dk[cc * TOK:(cc + 1) * TOK]
                part[o, cc, 1, :, lanes_h] = dv[cc * TOK:(cc + 1) * TOK]
            dqacc[h] = dqacc[h] + dot_tn(keys(zi, 0, h), ds)

        for h in range(HEADS):
            body(h)

    def sib_copy(o, a):
        return rcopy(
            part.at[o, other, a], sib_recv.at[o, a], sib_ss.at[o, a], sib_rs.at[o, a], sib
        )

    def rs_copy(o, a):
        if a == 0:
            slot = o + 2
            off = jnp.where(lax.rem(o, 2) == 0, 1, -1)
        else:
            slot = jnp.where(o == 0, 1, o + 2)
            off = jnp.where((lax.rem(o, 2) == 0) & (o > 0), 1, -1)
        return rcopy(
            rs_send.at[o, a], rs_recv.at[slot, a], rs_ss.at[o, a], rs_rs.at[slot, a], z_dev(off)
        )

    def rs_wait(o, a):
        slot = rs_recv.at[o, a]
        rcopy(slot, slot, rs_ss.at[0, a], rs_rs.at[o, a], up).wait_recv()

    def finalize(o, a):
        sib_copy(o, a).wait_recv()
        total = part[o, core, a].astype(F32) + sib_recv[o, a].astype(F32)
        if o >= 2 + a or (a == 1 and o == 1):
            rs_wait(o, a)
            total = total + rs_recv[o, a].astype(F32)
        rs_send[o, a] = total.astype(BF16)
        rs_copy(o, a).start()

    def bwd_range(first, last):
        def body(o, carry):
            bwd(o)
            for a in range(2):
                sib_copy(o, a).start()
            return carry

        lax.fori_loop(first, last, body, 0)

    turns = (
        ((0, 0), (0, 1)), ((1, 0), (2, 1)), ((1, 1), (2, 0)), ((3, 0), (4, 1)),
        ((3, 1), (4, 0)), ((5, 0), (6, 1)), ((5, 1), (6, 0)),
    )

    def turn_out(n):
        for o, a in turns[n]:
            finalize(o, a)

    bwd_range(0, 2)
    turn_out(0)
    bwd_range(2, 4)
    turn_out(1)

    own_stats = st_recv[:, 0:HEADS, pl.ds(pl.multiple_of(x * TOK, TOK), TOK)]
    own_top = jnp.max(own_stats, axis=0)
    own_w = jnp.exp2(own_stats - own_top[None])
    own_w = own_w / jnp.sum(own_w, axis=0)[None]

    for h in range(HEADS):
        o_t = jnp.zeros((HD, TOK), F32)
        for i in range(1, X):
            o_piece(i, h, lax.rem(x + X - i, X), 0).wait_recv()
        for xx in range(X):
            o_t = o_t + o_recv[xx, h * HD:(h + 1) * HD, :].astype(F32) * own_w[xx, h:h + 1]
        attb[x, h] = o_t.T.astype(BF16)
        for i in range(1, X):
            go(att_piece(i, h, x))
    bwd_range(4, 7)
    turn_out(2)
    bwd_range(7, Z)

    for h in range(HEADS):
        dq_h = (dqacc[h] * SCALE).astype(BF16)
        for xx in range(X):
            dq_send[xx, h * HD:(h + 1) * HD, :] = dq_h[:, xx * TOK:(xx + 1) * TOK]
    for i in range(1, X):
        x_send(4, i, dq_send.at[lax.rem(x + i, X)], dq_recv)
    dq_recv[x] = dq_send[x]

    turn_out(3)

    att = jnp.concatenate([attb[x, h] for h in range(HEADS)], axis=1)
    for i in range(1, Y):
        dst_y = lax.rem(y + i, Y)
        w_rows = wbuf[pl.ds(pl.multiple_of(dst_y * gcols, gcols), gcols), :]
        pj_send[dst_y] = dot_nt(att, w_rows).astype(BF16)
        y_send(2, i, pj_send.at[dst_y], pj_recv)
    w_rows = wbuf[pl.ds(pl.multiple_of(y * gcols, gcols), gcols), :]
    pj_recv[y] = dot_nt(att, w_rows).astype(BF16)
    turn_out(4)

    for hf in range(2):
        for i in range(1, X):
            gx_half(i, hf, None, lax.rem(x + X - i, X)).wait_recv()
    for h in range(HEADS):
        for i in range(1, X):
            att_piece(i, h, lax.rem(x + X - i, X)).wait_recv()
    att_all = jnp.concatenate(
        [attb[:, h].reshape(QN, HD) for h in range(HEADS)], axis=1
    )

    def gw_body(j, carry):
        lanes_j = pl.ds(pl.multiple_of(j * 128, 128), 128)
        left = gpx[:, :, lanes_j].reshape(QN, 128)
        gwf[pl.ds(pl.multiple_of(j * 128, 128), 128), :] = dot_tn(left, att_all)
        return carry

    lax.fori_loop(0, gcols // 128, gw_body, 0)
    grow = gw_out.shape[0]
    for zz in range(Z):
        for cc in range(2):
            first = (zz * 2 + cc) * grow
            gwp[cc, zz] = gwf[first:first + grow, :].astype(BF16)
    gsib = rcopy(gwp.at[other], g_sib, gsib_ss, gsib_rs, sib)
    go(gsib)

    turn_out(5)

    def g_copy(idx, off):
        return rcopy(g_send.at[idx], g_recv.at[idx], g_ss.at[idx], g_rs.at[idx], z_dev(off))

    def g_term(off):
        zi = zmod(off)
        return gwp[core, zi].astype(F32) + g_sib[zi].astype(F32)

    def g_get(idx):
        g_copy(idx, 1).wait_recv()
        return g_recv[idx].astype(F32)

    gsib.wait_recv()
    for idx, off, to in ((0, 4, 2), (1, 3, 1), (2, -3, -1), (3, 1, 1), (4, -1, -1)):
        g_send[idx] = g_term(off).astype(BF16)
        go(g_copy(idx, to))
    turn_out(6)
    g_send[5] = (g_term(2) + g_get(0) + g_get(1)).astype(BF16)
    go(g_copy(5, 2))
    g_send[6] = (g_term(-2) + g_get(2)).astype(BF16)
    go(g_copy(6, -2))

    for i in range(1, Y):
        y_recv(2, i, pj_recv)
    proj = pj_recv[0].astype(F32)
    for yy in range(1, Y):
        proj = proj + pj_recv[yy].astype(F32)
    proj_out[...] = proj.astype(BF16)
    for i in range(1, X):
        x_recv(4, i, dq_recv)
    for h in range(HEADS):
        dq_t = jnp.zeros((HD, TOK), F32)
        for xx in range(X):
            dq_t = dq_t + dq_recv[xx, h * HD:(h + 1) * HD, :].astype(F32)
        dq_out[:, h * HD:(h + 1) * HD] = dq_t.T.astype(BF16)
    gw_out[...] = g_term(0) + g_get(3) + g_get(4) + g_get(5) + g_get(6)
    last = Z - 1
    for a, out in ((0, dk_out), (1, dv_out)):
        sib_copy(last, a).wait_recv()
        rs_wait(last, a)
        rs_wait(last + 1, a)
        out[...] = (
            part[last, core, a].astype(F32)
            + sib_recv[last, a].astype(F32)
            + rs_recv[last, a].astype(F32)
            + rs_recv[last + 1, a].astype(F32)
        ).astype(BF16)

    for copy in sends:
        copy.wait_send()
    for a in range(2):
        for o in range(Z):
            sib_copy(o, a).wait_send()
            if o < last:
                rs_copy(o, a).wait_send()


def finish(*refs):
    half = len(refs) // 2
    for src, out in zip(refs[:half], refs[half:]):
        out[...] = src[...]


def per_device(X, Z, Y, queries, key_rows, value_rows, out_weight, grad_projected, segment_len, block_order):
    gcols = grad_projected.shape[1]
    grow = out_weight.shape[0] // (X * Z * 2)
    QN = X * TOK
    vmem = pl.BlockSpec(memory_space=pltpu.VMEM)
    smem = pl.BlockSpec(memory_space=pltpu.SMEM)
    dma = pltpu.SemaphoreType.DMA
    scratch = [
        pltpu.VMEM((X, TOK, WID), BF16),
        pltpu.VMEM((X, TOK, WID), BF16),
        pltpu.VMEM((Z, 2, 2, TOK, WID), BF16),
        pltpu.VMEM((Y, TOK, gcols), BF16),
        pltpu.VMEM((X, TOK, gcols), BF16),
        pltpu.VMEM((Z, 2 * TOK, 128), jnp.int32),
        pltpu.VMEM((1, QN), jnp.int32),
        pltpu.VMEM((HEADS, Z, 2 * TOK, QN), F32),
        pltpu.VMEM((HEADS, Z, 2 * TOK, QN), F32),
        pltpu.VMEM((HEADS, Z, 1, QN), F32),
        pltpu.VMEM((HEADS, Z, 1, QN), F32),
        pltpu.VMEM((HEADS, Z, 1, QN), F32),
        pltpu.VMEM((HEADS, HD, QN), F32),
        pltpu.VMEM((HEADS, 1, QN), F32),
        pltpu.VMEM((8, QN), F32),
        pltpu.VMEM((X, 8, QN), F32),
        pltpu.VMEM(out_weight.shape, BF16),
        pltpu.VMEM((X, WID, TOK), BF16),
        pltpu.VMEM((X, WID, TOK), BF16),
        pltpu.VMEM((X, HEADS, TOK, HD), BF16),
        pltpu.VMEM((HEADS, HD, QN), F32),
        pltpu.VMEM((X, WID, TOK), BF16),
        pltpu.VMEM((X, WID, TOK), BF16),
        pltpu.VMEM((Y, TOK, gcols), BF16),
        pltpu.VMEM((Y, TOK, gcols), BF16),
        pltpu.VMEM((HEADS, Z, 1, QN), F32),
        pltpu.VMEM((HEADS, 1, QN), F32),
        pltpu.VMEM((Z, 2, 2, TOK, WID), BF16),
        pltpu.VMEM((Z, 2, TOK, WID), BF16),
        pltpu.VMEM((Z, 2, TOK, WID), BF16),
        pltpu.VMEM((Z + 1, 2, TOK, WID), BF16),
        pltpu.VMEM((gcols, WID), F32),
        pltpu.VMEM((2, Z, grow, WID), BF16),
        pltpu.VMEM((Z, grow, WID), BF16),
        pltpu.VMEM((Z, grow, WID), BF16),
        pltpu.VMEM((Z, grow, WID), BF16),
        dma,
        dma((11, X)), dma((11, X)),
        dma((X, 2)), dma((X, 2)),
        dma((3, Y)), dma((3, Y)),
        dma((2, Z // 2, 2)), dma((2, Z // 2, 2)),
        dma((Z, 2)), dma((Z, 2)),
        dma((Z, 2)), dma((Z, 2)),
        dma((Z + 1, 2)), dma((Z + 1, 2)),
        dma, dma,
        dma((Z,)), dma((Z,)),
    ]
    out_shape = (
        jax.ShapeDtypeStruct((TOK, gcols), BF16),
        jax.ShapeDtypeStruct((TOK, WID), BF16),
        jax.ShapeDtypeStruct((TOK, WID), BF16),
        jax.ShapeDtypeStruct((TOK, WID), BF16),
        jax.ShapeDtypeStruct((grow, WID), F32),
    )
    results = pl.pallas_call(
        functools.partial(kernel, X, Z, Y),
        out_shape=out_shape,
        in_specs=[smem, smem, vmem, vmem, vmem, pl.BlockSpec(memory_space=pl.ANY), vmem],
        out_specs=(vmem,) * 5,
        scratch_shapes=scratch,
        compiler_params=pltpu.CompilerParams(
            collective_id=0, has_side_effects=True, vmem_limit_bytes=60 * 1024 * 1024
        ),
        name="segment_attention",
    )(segment_len, block_order, queries, key_rows, value_rows, out_weight, grad_projected)
    return pl.pallas_call(
        finish,
        out_shape=out_shape,
        in_specs=[vmem] * 5,
        out_specs=(vmem,) * 5,
        name="outputs",
    )(*results)


def solution(mesh):
    ctx = mesh.shape["ctx"]
    Y = mesh.shape["head"]
    X = Y
    Z = ctx // (2 * X)
    return jax.shard_map(
        functools.partial(per_device, X, Z, Y),
        mesh=mesh,
        in_specs=(
            P("ctx", "head"),
            P("ctx", "head"),
            P("ctx", "head"),
            P(None, "head"),
            P("ctx", "head"),
            P(),
            P(),
        ),
        out_specs=(P("ctx", "head"),) * 5,
        check_vma=False,
    )
```

```python
import functools
import math

import jax
import jax.numpy as jnp
from jax import lax
from jax.experimental import pallas as pl
from jax.experimental.pallas import tpu as pltpu
from jax.sharding import PartitionSpec as P

HD = 128
HEADS = 3
TOK = 128
WID = HEADS * HD
BLK = 64
SEGS = 8
SCALE = 1.0 / math.sqrt(HD)
EXP2_SCALE = SCALE * math.log2(math.e)
NEG_FILL = -1e30
MAX_FLOOR = -1e20
F32 = jnp.float32
BF16 = jnp.bfloat16
MESH = pl.DeviceIdType.MESH


def dot_nn(a, b):
    return jnp.dot(a, b, preferred_element_type=F32)


def dot_nt(a, b):
    return lax.dot_general(a, b, (((1,), (1,)), ((), ())), preferred_element_type=F32)


def dot_tn(a, b):
    return lax.dot_general(a, b, (((0,), (0,)), ((), ())), preferred_element_type=F32)


def head_lanes(h):
    return slice(h * HD, (h + 1) * HD)


def kernel(
    X, Z, Y,
    seg_len, order, q_hbm, k_hbm, v_hbm, w_hbm, gp_hbm,
    proj_out, dq_out, dk_out, dv_out, gw_out,
    qb, db, kvb, gpf, gpx, segk, segq, pbuf, dpbuf, mst, lst, dst,
    oacc, mrun, st_send, st_recv, wbuf, o_send, o_recv, attb, dqacc, dq_send, dq_recv,
    pj_send, pj_recv, fac, delta, part, sib_recv, rs_send, rs_recv,
    gwf, gwp, g_sib, g_send, g_recv,
    w_sem,
    x_ss, x_rs, gx_ss, gx_rs, y_ss, y_rs, ring_ss, ring_rs, ksib_ss, ksib_rs,
    sib_ss, sib_rs, rs_ss, rs_rs, gsib_ss, gsib_rs, g_ss, g_rs,
):
    nplus, nminus = Z // 2, Z - 1 - Z // 2
    QN = X * TOK
    gcols = gp_hbm.shape[1]
    me = lax.axis_index("ctx")
    y = lax.axis_index("head")
    core = lax.rem(me, 2)
    z = lax.rem(me // 2, Z)
    x = me // (2 * Z)

    def ctx_of(xx, zz, cc):
        return (xx * Z + zz) * 2 + cc

    def zmod(off):
        return lax.rem(z + off + 2 * Z, Z)

    other = 1 - core
    sib = (ctx_of(x, z, other), y)
    up = (ctx_of(x, zmod(1), core), y)
    down = (ctx_of(x, zmod(-1), core), y)

    def x_dev(i):
        return (ctx_of(lax.rem(x + i, X), z, core), y)

    def y_dev(i):
        return (me, lax.rem(y + i, Y))

    def z_dev(i):
        return (ctx_of(x, zmod(i), core), y)

    def rcopy(src, dst_ref, ss, rs, dev):
        return pltpu.make_async_remote_copy(
            src_ref=src, dst_ref=dst_ref, send_sem=ss, recv_sem=rs,
            device_id=dev, device_id_type=MESH,
        )

    barrier = pltpu.get_barrier_semaphore()
    partners = [sib] + [z_dev(i) for i in (1, -1, 2, -2)]
    partners += [x_dev(i) for i in range(1, X)] + [y_dev(i) for i in range(1, Y)]
    for dev in partners:
        pl.semaphore_signal(barrier, inc=1, device_id=dev, device_id_type=MESH)
    local = [
        pltpu.make_async_copy(src, dst_ref, w_sem.at[i])
        for i, (src, dst_ref) in enumerate((
            (gp_hbm, gpf.at[y]), (k_hbm, kvb.at[z, core, 0]), (v_hbm, kvb.at[z, core, 1]),
            (q_hbm, qb.at[x]), (w_hbm, wbuf),
        ))
    ]
    for copy in local:
        copy.start()

    sends = []

    def go(copy):
        copy.start()
        sends.append(copy)

    def x_recv(kind, i, buf):
        slot = buf.at[lax.rem(x + X - i, X)]
        rcopy(slot, slot, x_ss.at[kind, i], x_rs.at[kind, i], x_dev(i)).wait_recv()

    def x_send(kind, i, src, buf):
        go(rcopy(src, buf.at[x], x_ss.at[kind, i], x_rs.at[kind, i], x_dev(i)))

    def y_recv(kind, i, buf):
        slot = buf.at[lax.rem(y + Y - i, Y)]
        rcopy(slot, slot, y_ss.at[kind, i], y_rs.at[kind, i], y_dev(i)).wait_recv()

    def y_send(kind, i, src, buf):
        go(rcopy(src, buf.at[y], y_ss.at[kind, i], y_rs.at[kind, i], y_dev(i)))

    half = TOK // 2

    def rows_of(hf):
        return pl.ds(hf * half, half)

    def x_half(kind, i, hf, src_dev):
        slot = db.at[src_dev, rows_of(hf)]
        return rcopy(slot, slot, x_ss.at[kind, i], x_rs.at[kind, i], x_dev(i))

    def gx_half(i, hf, src, src_dev):
        slot = gpx.at[src_dev, rows_of(hf)]
        src = slot if src is None else src
        return rcopy(src, slot, gx_ss.at[i, hf], gx_rs.at[i, hf], x_dev(i))

    def o_piece(i, h, src_dev, dst_dev):
        rows_h = pl.ds(h * HD, HD)
        return rcopy(
            o_send.at[dst_dev, rows_h], o_recv.at[src_dev, rows_h],
            x_ss.at[5 + h, i], x_rs.at[5 + h, i], x_dev(i),
        )

    def att_piece(i, h, src_dev):
        slot = attb.at[src_dev, h]
        return rcopy(slot, slot, x_ss.at[8 + h, i], x_rs.at[8 + h, i], x_dev(i))

    def y_half(hf, i, src, src_dev):
        slot = gpf.at[src_dev, rows_of(hf)]
        return rcopy(src, slot, y_ss.at[hf, i], y_rs.at[hf, i], y_dev(i))

    def kv_slot(off, cc, a):
        return kvb.at[zmod(off), cc, a]

    def limit(direction, a):
        return nplus if direction == a else nminus

    def ring_send(direction, step, a, src):
        off = 1 - step if direction == 0 else step - 1
        go(rcopy(
            src, kv_slot(off, core, a),
            ring_ss.at[direction, step - 1, a], ring_rs.at[direction, step - 1, a],
            up if direction == 0 else down,
        ))

    def ring_wait(direction, step, a):
        off = -step if direction == 0 else step
        slot = kv_slot(off, core, a)
        rcopy(
            slot, slot, ring_ss.at[direction, step - 1, a],
            ring_rs.at[direction, step - 1, a], up,
        ).wait_recv()

    def sib_index(off):
        return nplus + off if off > 0 else -off

    def ksib_send(off, a, src):
        j = sib_index(off)
        go(rcopy(src, kv_slot(off, core, a), ksib_ss.at[j, a], ksib_rs.at[j, a], sib))

    def ksib_wait(off, a):
        j = sib_index(off)
        slot = kv_slot(off, other, a)
        rcopy(slot, slot, ksib_ss.at[j, a], ksib_rs.at[j, a], sib).wait_recv()

    ends = []
    total = seg_len[0]
    for i in range(SEGS - 1):
        ends.append(total)
        total = total + seg_len[i + 1]

    def segments(row_in_block, ctx_id):
        first = order[2 * ctx_id] * BLK
        second = order[2 * ctx_id + 1] * BLK - BLK
        pos = row_in_block + jnp.where(row_in_block < BLK, first, second)
        seg = jnp.zeros_like(pos)
        for end in ends:
            seg = seg + jnp.where(pos >= end, 1, 0)
        return seg

    lanes = lax.broadcasted_iota(jnp.int32, (1, TOK), 1)
    for xx in range(X):
        segq[:, xx * TOK:(xx + 1) * TOK] = segments(lanes, ctx_of(xx, z, core))
    rows = lax.broadcasted_iota(jnp.int32, (TOK, 128), 0)

    def seg_body(zz, carry):
        for cc in range(2):
            segk[zz, cc * TOK:(cc + 1) * TOK, :] = segments(rows, ctx_of(x, zz, cc))
        return carry

    lax.fori_loop(0, Z, seg_body, 0)
    for h in range(HEADS):
        mrun[h] = jnp.full((1, QN), MAX_FLOOR, F32)
        oacc[h] = jnp.zeros((HD, QN), F32)
        dqacc[h] = jnp.zeros((HD, QN), F32)

    for copy in local[:-1]:
        copy.wait()
    pl.semaphore_wait(barrier, len(partners))

    def send_gp(hf):
        for i in range(1, Y):
            go(y_half(hf, i, gpf.at[y, rows_of(hf)], y))

    send_gp(0)
    for turn in range(2):
        for direction in range(2):
            a = (direction + turn) % 2
            ring_send(direction, 1, a, kvb.at[z, core, a])
    for a in range(2):
        ksib_send(0, a, kvb.at[z, core, a])
    for i in range(1, X):
        x_send(0, i, qb.at[x], qb)
    send_gp(1)

    def keys(zi, a, h):
        return kvb[zi, :, a, :, head_lanes(h)].reshape(2 * TOK, HD)

    def gathered(buf, h):
        return buf[:, :, head_lanes(h)].reshape(QN, HD)

    def fwd(zi):
        def body(h):
            s = dot_nt(keys(zi, 0, h), gathered(qb, h))
            sk = jnp.concatenate([segk[zi]] * X, axis=1)
            s = jnp.where(sk <= segq[...], s, NEG_FILL)
            m = jnp.maximum(jnp.max(s, axis=0, keepdims=True), MAX_FLOOR)
            p = jnp.exp2((s - m) * EXP2_SCALE)
            pbuf[h, zi] = p
            mst[h, zi] = m
            lst[h, zi] = jnp.sum(p, axis=0, keepdims=True)
            pv = dot_tn(keys(zi, 1, h), p.astype(BF16))
            m_old = mrun[h]
            m_new = jnp.maximum(m_old, m)
            mrun[h] = m_new
            oacc[h] = (
                oacc[h] * jnp.exp2((m_old - m_new) * EXP2_SCALE)
                + pv * jnp.exp2((m - m_new) * EXP2_SCALE)
            )

        for h in range(HEADS):
            body(h)

    def dprob(zi):
        def body(h):
            dp = dot_nt(keys(zi, 1, h), gathered(db, h))
            dpbuf[h, zi] = dp
            dst[h, zi] = jnp.sum(dp * pbuf[h, zi], axis=0, keepdims=True)

        for h in range(HEADS):
            body(h)

    def ring_turn(step, turn):
        for direction in range(2):
            a = (direction + turn) % 2
            off = -step if direction == 0 else step
            far = limit(direction, a)
            if step <= far:
                ring_wait(direction, step, a)
                if step < far:
                    ring_send(direction, step + 1, a, kv_slot(off, core, a))
                ksib_send(-step if step == nplus else off, a, kv_slot(off, core, a))

    def fwd_at(off):
        for a in range(2):
            ksib_wait(off, a)
        fwd(zmod(off))

    def dprob_range(first, last):
        def body(i, carry):
            dprob(zmod(i))
            return carry

        lax.fori_loop(first, last, body, 0)

    def dout_half(hf):
        acc = None
        for i in range(Y):
            src_y = lax.rem(y + Y - i, Y)
            if i:
                y_half(hf, i, gpf.at[src_y, rows_of(hf)], src_y).wait_recv()
            w_rows = wbuf[pl.ds(pl.multiple_of(src_y * gcols, gcols), gcols), :]
            term = dot_nn(gpf[src_y, rows_of(hf), :], w_rows)
            acc = term if acc is None else acc + term
        db[x, rows_of(hf), :] = acc.astype(BF16)
        for i in range(1, X):
            go(x_half(1 + hf, i, hf, x))

    def send_gx():
        for hf in range(2):
            for i in range(1, X):
                go(gx_half(i, hf, gpf.at[lax.rem(x + i, X), rows_of(hf)], x))
        gpx[x] = gpf[x]

    local[-1].wait()
    ring_turn(1, 0)
    ring_turn(1, 1)
    dout_half(0)
    for i in range(1, X):
        x_recv(0, i, qb)
    fwd_at(0)
    ring_turn(2, 0)
    dout_half(1)
    ring_turn(2, 1)
    send_gx()
    fwd_at(-1)
    fwd_at(1)
    ring_turn(3, 0)
    fwd_at(-2)
    ring_turn(3, 1)
    fwd_at(2)
    fwd_at(-3)
    ring_turn(4, 0)
    fwd_at(3)
    fwd_at(-4)
    for hf in range(2):
        for i in range(1, X):
            x_half(1 + hf, i, hf, lax.rem(x + X - i, X)).wait_recv()
    dprob_range(0, Z)

    inverse = []
    for h in range(HEADS):
        m_top = mrun[h]
        w = jnp.exp2((mst[h] - m_top[None]) * EXP2_SCALE)
        l_sum = jnp.maximum(jnp.sum(lst[h] * w, axis=0), 1e-30)
        inv = 1.0 / l_sum
        inverse.append(inv)
        st_send[h:h + 1, :] = m_top * EXP2_SCALE + jnp.log2(l_sum)
        st_send[HEADS + h:HEADS + h + 1, :] = jnp.sum(dst[h] * w, axis=0) * inv
    st_send[2 * HEADS:8, :] = jnp.zeros((8 - 2 * HEADS, QN), F32)
    for i in range(1, X):
        x_send(3, i, st_send, st_recv)
    for h in range(HEADS):
        o_h = (oacc[h] * inverse[h]).astype(BF16)
        for xx in range(X):
            o_send[xx, h * HD:(h + 1) * HD, :] = o_h[:, xx * TOK:(xx + 1) * TOK]
        for i in range(1, X):
            go(o_piece(i, h, x, lax.rem(x + i, X)))
    st_recv[x] = st_send[...]
    o_recv[x] = o_send[x]
    for i in range(1, X):
        x_recv(3, i, st_recv)
    lse_all = st_recv[:, 0:HEADS, :]
    top = jnp.max(lse_all, axis=0)
    lse = top + jnp.log2(jnp.sum(jnp.exp2(lse_all - top[None]), axis=0))
    weight = jnp.exp2(lse_all - lse[None])
    for h in range(HEADS):
        fac[h] = jnp.exp2(mst[h] * EXP2_SCALE - lse[h:h + 1][None])
    delta_all = jnp.sum(weight * st_recv[:, HEADS:2 * HEADS, :], axis=0)
    for h in range(HEADS):
        delta[h] = delta_all[h:h + 1]
    def dest_off(o):
        pair = o // 2
        return jnp.where(lax.rem(o, 2) == 0, nplus - pair, pair - nminus)

    def bwd(o):
        zi = zmod(dest_off(o))

        def body(h):
            lanes_h = head_lanes(h)
            p = pbuf[h, zi] * fac[h, zi]
            ds = (p * (dpbuf[h, zi] - delta[h])).astype(BF16)
            dv = dot_nn(p.astype(BF16), gathered(db, h)).astype(BF16)
            dk = (dot_nn(ds, gathered(qb, h)) * SCALE).astype(BF16)
            for cc in range(2):
                part[o, cc, 0, :, lanes_h] = dk[cc * TOK:(cc + 1) * TOK]
                part[o, cc, 1, :, lanes_h] = dv[cc * TOK:(cc + 1) * TOK]
            dqacc[h] = dqacc[h] + dot_tn(keys(zi, 0, h), ds)

        for h in range(HEADS):
            body(h)

    def sib_copy(o, a):
        return rcopy(
            part.at[o, other, a], sib_recv.at[o, a], sib_ss.at[o, a], sib_rs.at[o, a], sib
        )

    def rs_copy(o, a):
        if a == 0:
            slot = o + 2
            off = jnp.where(lax.rem(o, 2) == 0, 1, -1)
        else:
            slot = jnp.where(o == 0, 1, o + 2)
            off = jnp.where((lax.rem(o, 2) == 0) & (o > 0), 1, -1)
        return rcopy(
            rs_send.at[o, a], rs_recv.at[slot, a], rs_ss.at[o, a], rs_rs.at[slot, a], z_dev(off)
        )

    def rs_wait(o, a):
        slot = rs_recv.at[o, a]
        rcopy(slot, slot, rs_ss.at[0, a], rs_rs.at[o, a], up).wait_recv()

    def finalize(o, a):
        sib_copy(o, a).wait_recv()
        total = part[o, core, a].astype(F32) + sib_recv[o, a].astype(F32)
        if o >= 2 + a or (a == 1 and o == 1):
            rs_wait(o, a)
            total = total + rs_recv[o, a].astype(F32)
        rs_send[o, a] = total.astype(BF16)
        rs_copy(o, a).start()

    def bwd_range(first, last):
        def body(o, carry):
            bwd(o)
            for a in range(2):
                sib_copy(o, a).start()
            return carry

        lax.fori_loop(first, last, body, 0)

    turns = (
        ((0, 0), (0, 1)), ((1, 0), (2, 1)), ((1, 1), (2, 0)), ((3, 0), (4, 1)),
        ((3, 1), (4, 0)), ((5, 0), (6, 1)), ((5, 1), (6, 0)),
    )

    def turn_out(n):
        for o, a in turns[n]:
            finalize(o, a)

    bwd_range(0, 2)
    turn_out(0)
    bwd_range(2, 4)
    turn_out(1)

    own_stats = st_recv[:, 0:HEADS, pl.ds(pl.multiple_of(x * TOK, TOK), TOK)]
    own_top = jnp.max(own_stats, axis=0)
    own_w = jnp.exp2(own_stats - own_top[None])
    own_w = own_w / jnp.sum(own_w, axis=0)[None]

    for h in range(HEADS):
        o_t = jnp.zeros((HD, TOK), F32)
        for i in range(1, X):
            o_piece(i, h, lax.rem(x + X - i, X), 0).wait_recv()
        for xx in range(X):
            o_t = o_t + o_recv[xx, h * HD:(h + 1) * HD, :].astype(F32) * own_w[xx, h:h + 1]
        attb[x, h] = o_t.T.astype(BF16)
        for i in range(1, X):
            go(att_piece(i, h, x))
    bwd_range(4, 7)
    turn_out(2)
    bwd_range(7, Z)

    for h in range(HEADS):
        dq_h = (dqacc[h] * SCALE).astype(BF16)
        for xx in range(X):
            dq_send[xx, h * HD:(h + 1) * HD, :] = dq_h[:, xx * TOK:(xx + 1) * TOK]
    for i in range(1, X):
        x_send(4, i, dq_send.at[lax.rem(x + i, X)], dq_recv)
    dq_recv[x] = dq_send[x]

    turn_out(3)

    att = jnp.concatenate([attb[x, h] for h in range(HEADS)], axis=1)
    for i in range(1, Y):
        dst_y = lax.rem(y + i, Y)
        w_rows = wbuf[pl.ds(pl.multiple_of(dst_y * gcols, gcols), gcols), :]
        pj_send[dst_y] = dot_nt(att, w_rows).astype(BF16)
        y_send(2, i, pj_send.at[dst_y], pj_recv)
    w_rows = wbuf[pl.ds(pl.multiple_of(y * gcols, gcols), gcols), :]
    pj_recv[y] = dot_nt(att, w_rows).astype(BF16)
    turn_out(4)

    for hf in range(2):
        for i in range(1, X):
            gx_half(i, hf, None, lax.rem(x + X - i, X)).wait_recv()
    for h in range(HEADS):
        for i in range(1, X):
            att_piece(i, h, lax.rem(x + X - i, X)).wait_recv()
    att_all = jnp.concatenate(
        [attb[:, h].reshape(QN, HD) for h in range(HEADS)], axis=1
    )

    def gw_body(j, carry):
        lanes_j = pl.ds(pl.multiple_of(j * 128, 128), 128)
        left = gpx[:, :, lanes_j].reshape(QN, 128)
        gwf[pl.ds(pl.multiple_of(j * 128, 128), 128), :] = dot_tn(left, att_all)
        return carry

    lax.fori_loop(0, gcols // 128, gw_body, 0)
    grow = gw_out.shape[0]
    for zz in range(Z):
        for cc in range(2):
            first = (zz * 2 + cc) * grow
            gwp[cc, zz] = gwf[first:first + grow, :].astype(BF16)
    gsib = rcopy(gwp.at[other], g_sib, gsib_ss, gsib_rs, sib)
    go(gsib)

    turn_out(5)

    def g_copy(idx, off):
        return rcopy(g_send.at[idx], g_recv.at[idx], g_ss.at[idx], g_rs.at[idx], z_dev(off))

    def g_term(off):
        zi = zmod(off)
        return gwp[core, zi].astype(F32) + g_sib[zi].astype(F32)

    def g_get(idx):
        g_copy(idx, 1).wait_recv()
        return g_recv[idx].astype(F32)

    gsib.wait_recv()
    for idx, off, to in ((0, 4, 2), (1, 3, 1), (2, -3, -1), (3, 1, 1), (4, -1, -1)):
        g_send[idx] = g_term(off).astype(BF16)
        go(g_copy(idx, to))
    turn_out(6)
    g_send[5] = (g_term(2) + g_get(0) + g_get(1)).astype(BF16)
    go(g_copy(5, 2))
    g_send[6] = (g_term(-2) + g_get(2)).astype(BF16)
    go(g_copy(6, -2))

    for i in range(1, Y):
        y_recv(2, i, pj_recv)
    proj = pj_recv[0].astype(F32)
    for yy in range(1, Y):
        proj = proj + pj_recv[yy].astype(F32)
    proj_out[...] = proj.astype(BF16)
    for i in range(1, X):
        x_recv(4, i, dq_recv)
    for h in range(HEADS):
        dq_t = jnp.zeros((HD, TOK), F32)
        for xx in range(X):
            dq_t = dq_t + dq_recv[xx, h * HD:(h + 1) * HD, :].astype(F32)
        dq_out[:, h * HD:(h + 1) * HD] = dq_t.T.astype(BF16)
    gw_out[...] = g_term(0) + g_get(3) + g_get(4) + g_get(5) + g_get(6)
    last = Z - 1
    for a, out in ((0, dk_out), (1, dv_out)):
        sib_copy(last, a).wait_recv()
        rs_wait(last, a)
        rs_wait(last + 1, a)
        out[...] = (
            part[last, core, a].astype(F32)
            + sib_recv[last, a].astype(F32)
            + rs_recv[last, a].astype(F32)
            + rs_recv[last + 1, a].astype(F32)
        ).astype(BF16)

    for copy in sends:
        copy.wait_send()
    for a in range(2):
        for o in range(Z):
            sib_copy(o, a).wait_send()
            if o < last:
                rs_copy(o, a).wait_send()


def finish(*refs):
    half = len(refs) // 2
    for src, out in zip(refs[:half], refs[half:]):
        out[...] = src[...]


def per_device(X, Z, Y, queries, key_rows, value_rows, out_weight, grad_projected, segment_len, block_order):
    gcols = grad_projected.shape[1]
    grow = out_weight.shape[0] // (X * Z * 2)
    QN = X * TOK
    vmem = pl.BlockSpec(memory_space=pltpu.VMEM)
    smem = pl.BlockSpec(memory_space=pltpu.SMEM)
    dma = pltpu.SemaphoreType.DMA
    scratch = [
        pltpu.VMEM((X, TOK, WID), BF16),
        pltpu.VMEM((X, TOK, WID), BF16),
        pltpu.VMEM((Z, 2, 2, TOK, WID), BF16),
        pltpu.VMEM((Y, TOK, gcols), BF16),
        pltpu.VMEM((X, TOK, gcols), BF16),
        pltpu.VMEM((Z, 2 * TOK, 128), jnp.int32),
        pltpu.VMEM((1, QN), jnp.int32),
        pltpu.VMEM((HEADS, Z, 2 * TOK, QN), F32),
        pltpu.VMEM((HEADS, Z, 2 * TOK, QN), F32),
        pltpu.VMEM((HEADS, Z, 1, QN), F32),
        pltpu.VMEM((HEADS, Z, 1, QN), F32),
        pltpu.VMEM((HEADS, Z, 1, QN), F32),
        pltpu.VMEM((HEADS, HD, QN), F32),
        pltpu.VMEM((HEADS, 1, QN), F32),
        pltpu.VMEM((8, QN), F32),
        pltpu.VMEM((X, 8, QN), F32),
        pltpu.VMEM(out_weight.shape, BF16),
        pltpu.VMEM((X, WID, TOK), BF16),
        pltpu.VMEM((X, WID, TOK), BF16),
        pltpu.VMEM((X, HEADS, TOK, HD), BF16),
        pltpu.VMEM((HEADS, HD, QN), F32),
        pltpu.VMEM((X, WID, TOK), BF16),
        pltpu.VMEM((X, WID, TOK), BF16),
        pltpu.VMEM((Y, TOK, gcols), BF16),
        pltpu.VMEM((Y, TOK, gcols), BF16),
        pltpu.VMEM((HEADS, Z, 1, QN), F32),
        pltpu.VMEM((HEADS, 1, QN), F32),
        pltpu.VMEM((Z, 2, 2, TOK, WID), BF16),
        pltpu.VMEM((Z, 2, TOK, WID), BF16),
        pltpu.VMEM((Z, 2, TOK, WID), BF16),
        pltpu.VMEM((Z + 1, 2, TOK, WID), BF16),
        pltpu.VMEM((gcols, WID), F32),
        pltpu.VMEM((2, Z, grow, WID), BF16),
        pltpu.VMEM((Z, grow, WID), BF16),
        pltpu.VMEM((Z, grow, WID), BF16),
        pltpu.VMEM((Z, grow, WID), BF16),
        dma((5,)),
        dma((11, X)), dma((11, X)),
        dma((X, 2)), dma((X, 2)),
        dma((3, Y)), dma((3, Y)),
        dma((2, Z // 2, 2)), dma((2, Z // 2, 2)),
        dma((Z, 2)), dma((Z, 2)),
        dma((Z, 2)), dma((Z, 2)),
        dma((Z + 1, 2)), dma((Z + 1, 2)),
        dma, dma,
        dma((Z,)), dma((Z,)),
    ]
    out_shape = (
        jax.ShapeDtypeStruct((TOK, gcols), BF16),
        jax.ShapeDtypeStruct((TOK, WID), BF16),
        jax.ShapeDtypeStruct((TOK, WID), BF16),
        jax.ShapeDtypeStruct((TOK, WID), BF16),
        jax.ShapeDtypeStruct((grow, WID), F32),
    )
    results = pl.pallas_call(
        functools.partial(kernel, X, Z, Y),
        out_shape=out_shape,
        in_specs=[smem, smem] + [pl.BlockSpec(memory_space=pl.ANY)] * 5,
        out_specs=(vmem,) * 5,
        scratch_shapes=scratch,
        compiler_params=pltpu.CompilerParams(
            collective_id=0, has_side_effects=True, vmem_limit_bytes=60 * 1024 * 1024
        ),
        name="segment_attention",
    )(segment_len, block_order, queries, key_rows, value_rows, out_weight, grad_projected)
    return pl.pallas_call(
        finish,
        out_shape=out_shape,
        in_specs=[vmem] * 5,
        out_specs=(vmem,) * 5,
        name="outputs",
    )(*results)


def solution(mesh):
    ctx = mesh.shape["ctx"]
    Y = mesh.shape["head"]
    X = Y
    Z = ctx // (2 * X)
    return jax.shard_map(
        functools.partial(per_device, X, Z, Y),
        mesh=mesh,
        in_specs=(
            P("ctx", "head"),
            P("ctx", "head"),
            P("ctx", "head"),
            P(None, "head"),
            P("ctx", "head"),
            P(),
            P(),
        ),
        out_specs=(P("ctx", "head"),) * 5,
        check_vma=False,
    )
```

```python
import functools
import math

import jax
import jax.numpy as jnp
from jax import lax
from jax.experimental import pallas as pl
from jax.experimental.pallas import tpu as pltpu
from jax.sharding import PartitionSpec as P

HD = 128
HEADS = 3
TOK = 128
WID = HEADS * HD
BLK = 64
SEGS = 8
SCALE = 1.0 / math.sqrt(HD)
EXP2_SCALE = SCALE * math.log2(math.e)
NEG_FILL = -1e30
MAX_FLOOR = -1e20
F32 = jnp.float32
BF16 = jnp.bfloat16
MESH = pl.DeviceIdType.MESH


def dot_nn(a, b):
    return jnp.dot(a, b, preferred_element_type=F32)


def dot_nt(a, b):
    return lax.dot_general(a, b, (((1,), (1,)), ((), ())), preferred_element_type=F32)


def dot_tn(a, b):
    return lax.dot_general(a, b, (((0,), (0,)), ((), ())), preferred_element_type=F32)


def head_lanes(h):
    return slice(h * HD, (h + 1) * HD)


def kernel(
    X, Z, Y,
    seg_len, order, q_hbm, k_hbm, v_hbm, w_hbm, gp_hbm,
    proj_out, dq_out, dk_out, dv_out, gw_out,
    qb, db, kvb, gpf, gpx, segk, segq, pbuf, dpbuf, mst, lst, dst,
    oacc, mrun, st_send, st_recv, wbuf, o_send, o_recv, attb, dqacc, dq_send, dq_recv,
    pj_send, pj_recv, fac, delta, part, sib_recv, rs_send, rs_recv,
    gwf, gwp, g_sib, g_send, g_recv,
    w_sem,
    x_ss, x_rs, gx_ss, gx_rs, y_ss, y_rs, ring_ss, ring_rs, ksib_ss, ksib_rs,
    sib_ss, sib_rs, rs_ss, rs_rs, gsib_ss, gsib_rs, g_ss, g_rs,
):
    nplus, nminus = Z // 2, Z - 1 - Z // 2
    QN = X * TOK
    gcols = gp_hbm.shape[1]
    me = lax.axis_index("ctx")
    y = lax.axis_index("head")
    core = lax.rem(me, 2)
    z = lax.rem(me // 2, Z)
    x = me // (2 * Z)

    def ctx_of(xx, zz, cc):
        return (xx * Z + zz) * 2 + cc

    def zmod(off):
        return lax.rem(z + off + 2 * Z, Z)

    other = 1 - core
    sib = (ctx_of(x, z, other), y)
    up = (ctx_of(x, zmod(1), core), y)
    down = (ctx_of(x, zmod(-1), core), y)

    def x_dev(i):
        return (ctx_of(lax.rem(x + i, X), z, core), y)

    def y_dev(i):
        return (me, lax.rem(y + i, Y))

    def z_dev(i):
        return (ctx_of(x, zmod(i), core), y)

    def rcopy(src, dst_ref, ss, rs, dev):
        return pltpu.make_async_remote_copy(
            src_ref=src, dst_ref=dst_ref, send_sem=ss, recv_sem=rs,
            device_id=dev, device_id_type=MESH,
        )

    barrier = pltpu.get_barrier_semaphore()
    partners = [sib] + [z_dev(i) for i in (1, -1, 2, -2)]
    partners += [x_dev(i) for i in range(1, X)] + [y_dev(i) for i in range(1, Y)]
    for dev in partners:
        pl.semaphore_signal(barrier, inc=1, device_id=dev, device_id_type=MESH)
    local = [
        pltpu.make_async_copy(src, dst_ref, w_sem.at[i])
        for i, (src, dst_ref) in enumerate((
            (gp_hbm, gpf.at[y]), (k_hbm, kvb.at[z, core, 0]), (v_hbm, kvb.at[z, core, 1]),
            (q_hbm, qb.at[x]), (w_hbm, wbuf),
        ))
    ]
    for copy in local:
        copy.start()

    sends = []

    def go(copy):
        copy.start()
        sends.append(copy)

    def x_recv(kind, i, buf):
        slot = buf.at[lax.rem(x + X - i, X)]
        rcopy(slot, slot, x_ss.at[kind, i], x_rs.at[kind, i], x_dev(i)).wait_recv()

    def x_send(kind, i, src, buf):
        go(rcopy(src, buf.at[x], x_ss.at[kind, i], x_rs.at[kind, i], x_dev(i)))

    def y_recv(kind, i, buf):
        slot = buf.at[lax.rem(y + Y - i, Y)]
        rcopy(slot, slot, y_ss.at[kind, i], y_rs.at[kind, i], y_dev(i)).wait_recv()

    def y_send(kind, i, src, buf):
        go(rcopy(src, buf.at[y], y_ss.at[kind, i], y_rs.at[kind, i], y_dev(i)))

    half = TOK // 2

    def rows_of(hf):
        return pl.ds(hf * half, half)

    def x_half(kind, i, hf, src_dev):
        slot = db.at[src_dev, rows_of(hf)]
        return rcopy(slot, slot, x_ss.at[kind, i], x_rs.at[kind, i], x_dev(i))

    def gx_half(i, hf, src, src_dev):
        slot = gpx.at[src_dev, rows_of(hf)]
        src = slot if src is None else src
        return rcopy(src, slot, gx_ss.at[i, hf], gx_rs.at[i, hf], x_dev(i))

    def o_piece(i, h, src_dev, dst_dev):
        rows_h = pl.ds(h * HD, HD)
        return rcopy(
            o_send.at[dst_dev, rows_h], o_recv.at[src_dev, rows_h],
            x_ss.at[5 + h, i], x_rs.at[5 + h, i], x_dev(i),
        )

    def att_piece(i, h, src_dev):
        slot = attb.at[src_dev, h]
        return rcopy(slot, slot, x_ss.at[8 + h, i], x_rs.at[8 + h, i], x_dev(i))

    def y_half(hf, i, src, src_dev):
        slot = gpf.at[src_dev, rows_of(hf)]
        return rcopy(src, slot, y_ss.at[hf, i], y_rs.at[hf, i], y_dev(i))

    def kv_slot(off, cc, a):
        return kvb.at[zmod(off), cc, a]

    def limit(direction, a):
        return nplus if direction == a else nminus

    def ring_send(direction, step, a, src):
        off = 1 - step if direction == 0 else step - 1
        go(rcopy(
            src, kv_slot(off, core, a),
            ring_ss.at[direction, step - 1, a], ring_rs.at[direction, step - 1, a],
            up if direction == 0 else down,
        ))

    def ring_wait(direction, step, a):
        off = -step if direction == 0 else step
        slot = kv_slot(off, core, a)
        rcopy(
            slot, slot, ring_ss.at[direction, step - 1, a],
            ring_rs.at[direction, step - 1, a], up,
        ).wait_recv()

    def sib_index(off):
        return nplus + off if off > 0 else -off

    def ksib_send(off, a, src):
        j = sib_index(off)
        go(rcopy(src, kv_slot(off, core, a), ksib_ss.at[j, a], ksib_rs.at[j, a], sib))

    def ksib_wait(off, a):
        j = sib_index(off)
        slot = kv_slot(off, other, a)
        rcopy(slot, slot, ksib_ss.at[j, a], ksib_rs.at[j, a], sib).wait_recv()

    ends = []
    total = seg_len[0]
    for i in range(SEGS - 1):
        ends.append(total)
        total = total + seg_len[i + 1]

    def segments(row_in_block, ctx_id):
        first = order[2 * ctx_id] * BLK
        second = order[2 * ctx_id + 1] * BLK - BLK
        pos = row_in_block + jnp.where(row_in_block < BLK, first, second)
        seg = jnp.zeros_like(pos)
        for end in ends:
            seg = seg + jnp.where(pos >= end, 1, 0)
        return seg

    lanes = lax.broadcasted_iota(jnp.int32, (1, TOK), 1)
    for xx in range(X):
        segq[:, xx * TOK:(xx + 1) * TOK] = segments(lanes, ctx_of(xx, z, core))
    rows = lax.broadcasted_iota(jnp.int32, (TOK, 128), 0)

    def seg_body(zz, carry):
        for cc in range(2):
            segk[zz, cc * TOK:(cc + 1) * TOK, :] = segments(rows, ctx_of(x, zz, cc))
        return carry

    lax.fori_loop(0, Z, seg_body, 0)
    for h in range(HEADS):
        mrun[h] = jnp.full((1, QN), MAX_FLOOR, F32)
        oacc[h] = jnp.zeros((HD, QN), F32)
        dqacc[h] = jnp.zeros((HD, QN), F32)

    for copy in local[:-1]:
        copy.wait()
    pl.semaphore_wait(barrier, len(partners))

    def send_gp(hf):
        for i in range(1, Y):
            go(y_half(hf, i, gpf.at[y, rows_of(hf)], y))

    send_gp(0)
    for turn in range(2):
        for direction in range(2):
            a = (direction + turn) % 2
            ring_send(direction, 1, a, kvb.at[z, core, a])
    for a in range(2):
        ksib_send(0, a, kvb.at[z, core, a])
    for i in range(1, X):
        x_send(0, i, qb.at[x], qb)
    send_gp(1)

    def keys(zi, a, h):
        return kvb[zi, :, a, :, head_lanes(h)].reshape(2 * TOK, HD)

    def gathered(buf, h):
        return buf[:, :, head_lanes(h)].reshape(QN, HD)

    def fwd(zi):
        def body(h):
            s = dot_nt(keys(zi, 0, h), gathered(qb, h))
            sk = jnp.concatenate([segk[zi]] * X, axis=1)
            s = jnp.where(sk <= segq[...], s, NEG_FILL)
            m = jnp.maximum(jnp.max(s, axis=0, keepdims=True), MAX_FLOOR)
            p = jnp.exp2((s - m) * EXP2_SCALE)
            pbuf[h, zi] = p
            mst[h, zi] = m
            lst[h, zi] = jnp.sum(p, axis=0, keepdims=True)
            pv = dot_tn(keys(zi, 1, h), p.astype(BF16))
            m_old = mrun[h]
            m_new = jnp.maximum(m_old, m)
            mrun[h] = m_new
            oacc[h] = (
                oacc[h] * jnp.exp2((m_old - m_new) * EXP2_SCALE)
                + pv * jnp.exp2((m - m_new) * EXP2_SCALE)
            )

        for h in range(HEADS):
            body(h)

    def dprob(zi):
        def body(h):
            dp = dot_nt(keys(zi, 1, h), gathered(db, h))
            dpbuf[h, zi] = dp
            dst[h, zi] = jnp.sum(dp * pbuf[h, zi], axis=0, keepdims=True)

        for h in range(HEADS):
            body(h)

    def ring_turn(step, turn):
        for direction in range(2):
            a = (direction + turn) % 2
            off = -step if direction == 0 else step
            far = limit(direction, a)
            if step <= far:
                ring_wait(direction, step, a)
                if step < far:
                    ring_send(direction, step + 1, a, kv_slot(off, core, a))
                ksib_send(-step if step == nplus else off, a, kv_slot(off, core, a))

    def fwd_at(off):
        for a in range(2):
            ksib_wait(off, a)
        fwd(zmod(off))

    def dprob_range(first, last):
        def body(i, carry):
            dprob(zmod(i))
            return carry

        lax.fori_loop(first, last, body, 0)

    def dout_half(hf):
        acc = None
        for i in range(Y):
            src_y = lax.rem(y + Y - i, Y)
            if i:
                y_half(hf, i, gpf.at[src_y, rows_of(hf)], src_y).wait_recv()
            w_rows = wbuf[pl.ds(pl.multiple_of(src_y * gcols, gcols), gcols), :]
            term = dot_nn(gpf[src_y, rows_of(hf), :], w_rows)
            acc = term if acc is None else acc + term
        db[x, rows_of(hf), :] = acc.astype(BF16)
        for i in range(1, X):
            go(x_half(1 + hf, i, hf, x))

    def send_gx():
        for hf in range(2):
            for i in range(1, X):
                go(gx_half(i, hf, gpf.at[lax.rem(x + i, X), rows_of(hf)], x))
        gpx[x] = gpf[x]

    local[-1].wait()
    ring_turn(1, 0)
    ring_turn(1, 1)
    dout_half(0)
    for i in range(1, X):
        x_recv(0, i, qb)
    fwd_at(0)
    ring_turn(2, 0)
    dout_half(1)
    fwd_at(-1)
    ring_turn(2, 1)
    send_gx()
    fwd_at(1)
    fwd_at(-2)
    ring_turn(3, 0)
    fwd_at(2)
    ring_turn(3, 1)
    fwd_at(-3)
    fwd_at(3)
    ring_turn(4, 0)
    for hf in range(2):
        for i in range(1, X):
            x_half(1 + hf, i, hf, lax.rem(x + X - i, X)).wait_recv()
    dprob_range(Z - 2, Z + 3)
    fwd_at(-4)
    dprob_range(3, 6)

    inverse = []
    for h in range(HEADS):
        m_top = mrun[h]
        w = jnp.exp2((mst[h] - m_top[None]) * EXP2_SCALE)
        l_sum = jnp.maximum(jnp.sum(lst[h] * w, axis=0), 1e-30)
        inv = 1.0 / l_sum
        inverse.append(inv)
        st_send[h:h + 1, :] = m_top * EXP2_SCALE + jnp.log2(l_sum)
        st_send[HEADS + h:HEADS + h + 1, :] = jnp.sum(dst[h] * w, axis=0) * inv
    st_send[2 * HEADS:8, :] = jnp.zeros((8 - 2 * HEADS, QN), F32)
    for i in range(1, X):
        x_send(3, i, st_send, st_recv)
    for h in range(HEADS):
        o_h = (oacc[h] * inverse[h]).astype(BF16)
        for xx in range(X):
            o_send[xx, h * HD:(h + 1) * HD, :] = o_h[:, xx * TOK:(xx + 1) * TOK]
        for i in range(1, X):
            go(o_piece(i, h, x, lax.rem(x + i, X)))
    st_recv[x] = st_send[...]
    o_recv[x] = o_send[x]
    for i in range(1, X):
        x_recv(3, i, st_recv)
    lse_all = st_recv[:, 0:HEADS, :]
    top = jnp.max(lse_all, axis=0)
    lse = top + jnp.log2(jnp.sum(jnp.exp2(lse_all - top[None]), axis=0))
    weight = jnp.exp2(lse_all - lse[None])
    for h in range(HEADS):
        fac[h] = jnp.exp2(mst[h] * EXP2_SCALE - lse[h:h + 1][None])
    delta_all = jnp.sum(weight * st_recv[:, HEADS:2 * HEADS, :], axis=0)
    for h in range(HEADS):
        delta[h] = delta_all[h:h + 1]
    def dest_off(o):
        pair = o // 2
        return jnp.where(lax.rem(o, 2) == 0, nplus - pair, pair - nminus)

    def bwd(o):
        zi = zmod(dest_off(o))

        def body(h):
            lanes_h = head_lanes(h)
            p = pbuf[h, zi] * fac[h, zi]
            ds = (p * (dpbuf[h, zi] - delta[h])).astype(BF16)
            dv = dot_nn(p.astype(BF16), gathered(db, h)).astype(BF16)
            dk = (dot_nn(ds, gathered(qb, h)) * SCALE).astype(BF16)
            for cc in range(2):
                part[o, cc, 0, :, lanes_h] = dk[cc * TOK:(cc + 1) * TOK]
                part[o, cc, 1, :, lanes_h] = dv[cc * TOK:(cc + 1) * TOK]
            dqacc[h] = dqacc[h] + dot_tn(keys(zi, 0, h), ds)

        for h in range(HEADS):
            body(h)

    def sib_copy(o, a):
        return rcopy(
            part.at[o, other, a], sib_recv.at[o, a], sib_ss.at[o, a], sib_rs.at[o, a], sib
        )

    def rs_copy(o, a):
        if a == 0:
            slot = o + 2
            off = jnp.where(lax.rem(o, 2) == 0, 1, -1)
        else:
            slot = jnp.where(o == 0, 1, o + 2)
            off = jnp.where((lax.rem(o, 2) == 0) & (o > 0), 1, -1)
        return rcopy(
            rs_send.at[o, a], rs_recv.at[slot, a], rs_ss.at[o, a], rs_rs.at[slot, a], z_dev(off)
        )

    def rs_wait(o, a):
        slot = rs_recv.at[o, a]
        rcopy(slot, slot, rs_ss.at[0, a], rs_rs.at[o, a], up).wait_recv()

    def finalize(o, a):
        sib_copy(o, a).wait_recv()
        total = part[o, core, a].astype(F32) + sib_recv[o, a].astype(F32)
        if o >= 2 + a or (a == 1 and o == 1):
            rs_wait(o, a)
            total = total + rs_recv[o, a].astype(F32)
        rs_send[o, a] = total.astype(BF16)
        rs_copy(o, a).start()

    def bwd_range(first, last):
        def body(o, carry):
            bwd(o)
            for a in range(2):
                sib_copy(o, a).start()
            return carry

        lax.fori_loop(first, last, body, 0)

    turns = (
        ((0, 0), (0, 1)), ((1, 0), (2, 1)), ((1, 1), (2, 0)), ((3, 0), (4, 1)),
        ((3, 1), (4, 0)), ((5, 0), (6, 1)), ((5, 1), (6, 0)),
    )

    def turn_out(n):
        for o, a in turns[n]:
            finalize(o, a)

    bwd_range(0, 2)
    turn_out(0)
    bwd_range(2, 4)
    turn_out(1)

    own_stats = st_recv[:, 0:HEADS, pl.ds(pl.multiple_of(x * TOK, TOK), TOK)]
    own_top = jnp.max(own_stats, axis=0)
    own_w = jnp.exp2(own_stats - own_top[None])
    own_w = own_w / jnp.sum(own_w, axis=0)[None]

    for h in range(HEADS):
        o_t = jnp.zeros((HD, TOK), F32)
        for i in range(1, X):
            o_piece(i, h, lax.rem(x + X - i, X), 0).wait_recv()
        for xx in range(X):
            o_t = o_t + o_recv[xx, h * HD:(h + 1) * HD, :].astype(F32) * own_w[xx, h:h + 1]
        attb[x, h] = o_t.T.astype(BF16)
        for i in range(1, X):
            go(att_piece(i, h, x))
    bwd_range(4, 7)
    turn_out(2)
    bwd_range(7, Z)

    for h in range(HEADS):
        dq_h = (dqacc[h] * SCALE).astype(BF16)
        for xx in range(X):
            dq_send[xx, h * HD:(h + 1) * HD, :] = dq_h[:, xx * TOK:(xx + 1) * TOK]
    for i in range(1, X):
        x_send(4, i, dq_send.at[lax.rem(x + i, X)], dq_recv)
    dq_recv[x] = dq_send[x]

    turn_out(3)

    att = jnp.concatenate([attb[x, h] for h in range(HEADS)], axis=1)
    for i in range(1, Y):
        dst_y = lax.rem(y + i, Y)
        w_rows = wbuf[pl.ds(pl.multiple_of(dst_y * gcols, gcols), gcols), :]
        pj_send[dst_y] = dot_nt(att, w_rows).astype(BF16)
        y_send(2, i, pj_send.at[dst_y], pj_recv)
    w_rows = wbuf[pl.ds(pl.multiple_of(y * gcols, gcols), gcols), :]
    pj_recv[y] = dot_nt(att, w_rows).astype(BF16)
    turn_out(4)

    for hf in range(2):
        for i in range(1, X):
            gx_half(i, hf, None, lax.rem(x + X - i, X)).wait_recv()
    for h in range(HEADS):
        for i in range(1, X):
            att_piece(i, h, lax.rem(x + X - i, X)).wait_recv()
    att_all = jnp.concatenate(
        [attb[:, h].reshape(QN, HD) for h in range(HEADS)], axis=1
    )

    def gw_body(j, carry):
        lanes_j = pl.ds(pl.multiple_of(j * 128, 128), 128)
        left = gpx[:, :, lanes_j].reshape(QN, 128)
        gwf[pl.ds(pl.multiple_of(j * 128, 128), 128), :] = dot_tn(left, att_all)
        return carry

    lax.fori_loop(0, gcols // 128, gw_body, 0)
    grow = gw_out.shape[0]
    for zz in range(Z):
        for cc in range(2):
            first = (zz * 2 + cc) * grow
            gwp[cc, zz] = gwf[first:first + grow, :].astype(BF16)
    gsib = rcopy(gwp.at[other], g_sib, gsib_ss, gsib_rs, sib)
    go(gsib)

    turn_out(5)

    def g_copy(idx, off):
        return rcopy(g_send.at[idx], g_recv.at[idx], g_ss.at[idx], g_rs.at[idx], z_dev(off))

    def g_term(off):
        zi = zmod(off)
        return gwp[core, zi].astype(F32) + g_sib[zi].astype(F32)

    def g_get(idx):
        g_copy(idx, 1).wait_recv()
        return g_recv[idx].astype(F32)

    gsib.wait_recv()
    for idx, off, to in ((0, 4, 2), (1, 3, 1), (2, -3, -1), (3, 1, 1), (4, -1, -1)):
        g_send[idx] = g_term(off).astype(BF16)
        go(g_copy(idx, to))
    turn_out(6)
    g_send[5] = (g_term(2) + g_get(0) + g_get(1)).astype(BF16)
    go(g_copy(5, 2))
    g_send[6] = (g_term(-2) + g_get(2)).astype(BF16)
    go(g_copy(6, -2))

    for i in range(1, Y):
        y_recv(2, i, pj_recv)
    proj = pj_recv[0].astype(F32)
    for yy in range(1, Y):
        proj = proj + pj_recv[yy].astype(F32)
    proj_out[...] = proj.astype(BF16)
    for i in range(1, X):
        x_recv(4, i, dq_recv)
    for h in range(HEADS):
        dq_t = jnp.zeros((HD, TOK), F32)
        for xx in range(X):
            dq_t = dq_t + dq_recv[xx, h * HD:(h + 1) * HD, :].astype(F32)
        dq_out[:, h * HD:(h + 1) * HD] = dq_t.T.astype(BF16)
    gw_out[...] = g_term(0) + g_get(3) + g_get(4) + g_get(5) + g_get(6)
    last = Z - 1
    for a, out in ((0, dk_out), (1, dv_out)):
        sib_copy(last, a).wait_recv()
        rs_wait(last, a)
        rs_wait(last + 1, a)
        out[...] = (
            part[last, core, a].astype(F32)
            + sib_recv[last, a].astype(F32)
            + rs_recv[last, a].astype(F32)
            + rs_recv[last + 1, a].astype(F32)
        ).astype(BF16)

    for copy in sends:
        copy.wait_send()
    for a in range(2):
        for o in range(Z):
            sib_copy(o, a).wait_send()
            if o < last:
                rs_copy(o, a).wait_send()


def finish(*refs):
    half = len(refs) // 2
    for src, out in zip(refs[:half], refs[half:]):
        out[...] = src[...]


def per_device(X, Z, Y, queries, key_rows, value_rows, out_weight, grad_projected, segment_len, block_order):
    gcols = grad_projected.shape[1]
    grow = out_weight.shape[0] // (X * Z * 2)
    QN = X * TOK
    vmem = pl.BlockSpec(memory_space=pltpu.VMEM)
    smem = pl.BlockSpec(memory_space=pltpu.SMEM)
    dma = pltpu.SemaphoreType.DMA
    scratch = [
        pltpu.VMEM((X, TOK, WID), BF16),
        pltpu.VMEM((X, TOK, WID), BF16),
        pltpu.VMEM((Z, 2, 2, TOK, WID), BF16),
        pltpu.VMEM((Y, TOK, gcols), BF16),
        pltpu.VMEM((X, TOK, gcols), BF16),
        pltpu.VMEM((Z, 2 * TOK, 128), jnp.int32),
        pltpu.VMEM((1, QN), jnp.int32),
        pltpu.VMEM((HEADS, Z, 2 * TOK, QN), F32),
        pltpu.VMEM((HEADS, Z, 2 * TOK, QN), F32),
        pltpu.VMEM((HEADS, Z, 1, QN), F32),
        pltpu.VMEM((HEADS, Z, 1, QN), F32),
        pltpu.VMEM((HEADS, Z, 1, QN), F32),
        pltpu.VMEM((HEADS, HD, QN), F32),
        pltpu.VMEM((HEADS, 1, QN), F32),
        pltpu.VMEM((8, QN), F32),
        pltpu.VMEM((X, 8, QN), F32),
        pltpu.VMEM(out_weight.shape, BF16),
        pltpu.VMEM((X, WID, TOK), BF16),
        pltpu.VMEM((X, WID, TOK), BF16),
        pltpu.VMEM((X, HEADS, TOK, HD), BF16),
        pltpu.VMEM((HEADS, HD, QN), F32),
        pltpu.VMEM((X, WID, TOK), BF16),
        pltpu.VMEM((X, WID, TOK), BF16),
        pltpu.VMEM((Y, TOK, gcols), BF16),
        pltpu.VMEM((Y, TOK, gcols), BF16),
        pltpu.VMEM((HEADS, Z, 1, QN), F32),
        pltpu.VMEM((HEADS, 1, QN), F32),
        pltpu.VMEM((Z, 2, 2, TOK, WID), BF16),
        pltpu.VMEM((Z, 2, TOK, WID), BF16),
        pltpu.VMEM((Z, 2, TOK, WID), BF16),
        pltpu.VMEM((Z + 1, 2, TOK, WID), BF16),
        pltpu.VMEM((gcols, WID), F32),
        pltpu.VMEM((2, Z, grow, WID), BF16),
        pltpu.VMEM((Z, grow, WID), BF16),
        pltpu.VMEM((Z, grow, WID), BF16),
        pltpu.VMEM((Z, grow, WID), BF16),
        dma((5,)),
        dma((11, X)), dma((11, X)),
        dma((X, 2)), dma((X, 2)),
        dma((3, Y)), dma((3, Y)),
        dma((2, Z // 2, 2)), dma((2, Z // 2, 2)),
        dma((Z, 2)), dma((Z, 2)),
        dma((Z, 2)), dma((Z, 2)),
        dma((Z + 1, 2)), dma((Z + 1, 2)),
        dma, dma,
        dma((Z,)), dma((Z,)),
    ]
    out_shape = (
        jax.ShapeDtypeStruct((TOK, gcols), BF16),
        jax.ShapeDtypeStruct((TOK, WID), BF16),
        jax.ShapeDtypeStruct((TOK, WID), BF16),
        jax.ShapeDtypeStruct((TOK, WID), BF16),
        jax.ShapeDtypeStruct((grow, WID), F32),
    )
    results = pl.pallas_call(
        functools.partial(kernel, X, Z, Y),
        out_shape=out_shape,
        in_specs=[smem, smem] + [pl.BlockSpec(memory_space=pl.ANY)] * 5,
        out_specs=(vmem,) * 5,
        scratch_shapes=scratch,
        compiler_params=pltpu.CompilerParams(
            collective_id=0, has_side_effects=True, vmem_limit_bytes=60 * 1024 * 1024
        ),
        name="segment_attention",
    )(segment_len, block_order, queries, key_rows, value_rows, out_weight, grad_projected)
    return pl.pallas_call(
        finish,
        out_shape=out_shape,
        in_specs=[vmem] * 5,
        out_specs=(vmem,) * 5,
        name="outputs",
    )(*results)


def solution(mesh):
    ctx = mesh.shape["ctx"]
    Y = mesh.shape["head"]
    X = Y
    Z = ctx // (2 * X)
    return jax.shard_map(
        functools.partial(per_device, X, Z, Y),
        mesh=mesh,
        in_specs=(
            P("ctx", "head"),
            P("ctx", "head"),
            P("ctx", "head"),
            P(None, "head"),
            P("ctx", "head"),
            P(),
            P(),
        ),
        out_specs=(P("ctx", "head"),) * 5,
        check_vma=False,
    )
```
